32 devices in a mesh: dp: 2 (over y), ctx: 16 (over z, x, core).
Axes of the slice: x: 2, y: 2, z: 4, core: 2. Of those that a mesh axis runs over, the one named last changes fastest.
Arguments:
- layer_input: bfloat16 [2, 2048, 3072], P('dp', 'ctx'), may hold values from -6 to 6
- query_rows: bfloat16 [2, 2048, 3072], P('dp', 'ctx'), may hold values from -6 to 6
- key_rows: bfloat16 [2, 2048, 3072], P('dp', 'ctx'), may hold values from -6 to 6
- value_rows: bfloat16 [2, 2048, 3072], P('dp', 'ctx'), may hold values from -6 to 6
- out_grad: bfloat16 [2, 2048, 3072], P('dp', 'ctx'), may hold values from -6 to 6
Outputs:
- query_grad: bfloat16 [2, 2048, 3072], P('dp', 'ctx')
- key_grad: bfloat16 [2, 2048, 3072], P('dp', 'ctx')
- value_grad: bfloat16 [2, 2048, 3072], P('dp', 'ctx')
- key_weight_grad: float32 [3072, 3072], P('ctx', 'dp')
The draws below stay inside these ranges and needn't reach their ends.
All inputs are finite; a program needn't handle non-finite values.
Results may differ from the reference program's by a relative error of at most 0.028.
Values may be sent and summed in bfloat16 or wider, within the bound.
No kernel may reach another device: no remote copies, remote signals or barrier semaphores. Data moves between devices by JAX's collectives and lax.ppermute only.
A program may use at most 192 MiB of HBM per device.

```python
import jax
import jax.numpy as jnp
from jax import lax

DW = 3072
HEADS = 24
HEAD_DIM = 128
TOK_DEV = 128
HD = 3072
SEQS = 2
LENGTH = 2048
N_CTX = 16


def level_of(key, dims, shards, smallest, high):
    level = 1.0
    for axis_at, parts in shards:
        draws = jax.random.uniform(jax.random.fold_in(jax.random.fold_in(key, 6), axis_at), (parts,), jnp.float32, smallest / len(shards), high / len(shards))
        level = level * jnp.repeat(jnp.exp(draws), dims[axis_at] // parts).reshape((-1,) + (1,) * (len(dims) - 1 - axis_at))
    return level


def bell_draw(own_key, shape, scale, bound, cuts=(), held_as=jnp.bfloat16):
    values = jax.random.normal(own_key, shape, jnp.float32) * scale
    if len(cuts) > 0:
        values = level_of(own_key, shape, cuts, -0.22, 0.18) * values
    return jnp.clip(values, min=-bound, max=bound).astype(held_as)


def setup_inputs(seed: int = 0) -> dict:
    arg_keys = jax.random.split(jax.random.key(seed), 6)
    layer_input = bell_draw(arg_keys[0], (SEQS, LENGTH, DW), 1.0, 6.0, ((0, 2), (1, 16)))
    query_rows = bell_draw(arg_keys[1], (SEQS, LENGTH, HD), 1.0, 6.0, ((0, 2), (1, 16)))
    key_rows = bell_draw(arg_keys[2], (SEQS, LENGTH, HD), 1.0, 6.0, ((0, 2), (1, 16)))
    value_rows = bell_draw(arg_keys[3], (SEQS, LENGTH, HD), 1.0, 6.0, ((0, 2), (1, 16)))
    out_grad = bell_draw(arg_keys[4], (SEQS, LENGTH, HD), 1.0, 6.0, ((0, 2), (1, 16)))
    return {"layer_input": layer_input, "query_rows": query_rows, "key_rows": key_rows, "value_rows": value_rows, "out_grad": out_grad}


epsilon = 1e-05

def feature(values):
    wide = values.astype(jnp.float32)
    return jax.nn.elu(wide) + 1.0

def slope(values):
    wide = values.astype(jnp.float32)
    return jnp.where(wide > 0, 1.0, jnp.exp(jnp.minimum(wide, 0.0)))

def round_half(values):
    return lax.optimization_barrier(values.astype(jnp.bfloat16)).astype(jnp.float32)

def one_sequence(operands):
    query_rows, key_rows, value_rows, out_grad = operands
    shaped = (N_CTX, TOK_DEV, HEADS, HEAD_DIM)
    query = query_rows.reshape(shaped)
    keyed = key_rows.reshape(shaped)
    query_feature = round_half(feature(query))
    key_feature = round_half(feature(keyed))
    values = value_rows.reshape(shaped).astype(jnp.float32)
    upstream = out_grad.reshape(shaped).astype(jnp.float32)
    rows_index = lax.broadcasted_iota(jnp.int32, (TOK_DEV, TOK_DEV), 0)
    cols_index = lax.broadcasted_iota(jnp.int32, (TOK_DEV, TOK_DEV), 1)
    causal = (cols_index <= rows_index)[None, None]
    block_state = jnp.einsum('nthd,nthe->nhde', key_feature, values)
    prefix = jnp.cumsum(block_state, axis=0)
    state_in = round_half(jnp.concatenate([jnp.zeros_like(block_state[:1]), prefix[:-1]], axis=0))
    scores = jnp.einsum('nthd,nshd->nhts', query_feature, key_feature)
    scores = round_half(jnp.where(causal, scores, 0.0))
    output = jnp.einsum('nhts,nshe->nthe', scores, values) + jnp.einsum('nthd,nhde->nthe', query_feature, state_in)
    inverse_rms = lax.rsqrt(lax.optimization_barrier(jnp.mean(output * output, axis=-1, keepdims=True)) + epsilon)
    normed = output * inverse_rms
    projection = lax.optimization_barrier(jnp.mean(upstream * normed, axis=-1, keepdims=True))
    grad_output = round_half(inverse_rms * (upstream - normed * projection))
    block_grad = jnp.einsum('nthd,nthe->nhde', query_feature, grad_output)
    suffix = jnp.cumsum(block_grad[::-1], axis=0)[::-1]
    grad_in = round_half(jnp.concatenate([suffix[1:], jnp.zeros_like(block_grad[:1])], axis=0))
    grad_scores = jnp.einsum('nthe,nshe->nhts', grad_output, values)
    grad_scores = round_half(jnp.where(causal, grad_scores, 0.0))
    query_total = jnp.einsum('nhts,nshd->nthd', grad_scores, key_feature) + jnp.einsum('nthe,nhde->nthd', grad_output, state_in)
    key_total = jnp.einsum('nhts,nthd->nshd', grad_scores, query_feature) + jnp.einsum('nshe,nhde->nshd', values, grad_in)
    value_total = jnp.einsum('nhts,nthe->nshe', scores, grad_output) + jnp.einsum('nshd,nhde->nshe', key_feature, grad_in)
    query_grad = (query_total * slope(query)).astype(jnp.bfloat16).reshape(LENGTH, HD)
    key_grad = (key_total * slope(keyed)).astype(jnp.bfloat16).reshape(LENGTH, HD)
    value_grad = value_total.astype(jnp.bfloat16).reshape(LENGTH, HD)
    return (query_grad, key_grad, value_grad)

def reference(layer_input, query_rows, key_rows, value_rows, out_grad):
    query_grad, key_grad, value_grad = lax.map(one_sequence, (query_rows, key_rows, value_rows, out_grad))
    blocks_key = key_grad.reshape(SEQS * N_CTX, TOK_DEV, HD)
    blocks_input = layer_input.reshape(SEQS * N_CTX, TOK_DEV, DW)
    scale = (SEQS * LENGTH) ** (-0.5)

    def add_block(total, pair):
        piece = jnp.dot(pair[0].T, pair[1], preferred_element_type=jnp.float32)
        return (total + round_half(piece), None)
    result = lax.scan(add_block, jnp.zeros((HD, DW), jnp.float32), (blocks_key, blocks_input))
    weight_grad = result[0] * scale
    return (query_grad, key_grad, value_grad, weight_grad)
```

```python
import functools

import jax
import jax.numpy as jnp
from jax import lax
from jax.experimental import pallas as pl
from jax.experimental.pallas import tpu as pltpu
from jax.sharding import PartitionSpec as P

HEAD_DIM = 128
EPSILON = 1e-05
F32 = jnp.float32
BF16 = jnp.bfloat16

NN = (((1,), (0,)), ((), ()))
NT = (((1,), (1,)), ((), ()))
TN = (((0,), (0,)), ((), ()))


def dot(a, b, dims):
    return lax.dot_general(a, b, dims, preferred_element_type=F32)


def slope(values):
    wide = values.astype(F32)
    return jnp.where(wide > 0, 1.0, jnp.exp(jnp.minimum(wide, 0.0)))


def feature(values):
    wide = values.astype(F32)
    return jnp.where(wide > 0, wide + 1.0, jnp.exp(jnp.minimum(wide, 0.0))).astype(BF16)


def causal(rows):
    t = lax.broadcasted_iota(jnp.int32, (rows, rows), 0)
    s = lax.broadcasted_iota(jnp.int32, (rows, rows), 1)
    return s <= t


def heads_of(ref):
    for head in range(ref.shape[1] // HEAD_DIM):
        yield slice(head * HEAD_DIM, (head + 1) * HEAD_DIM)


def block_state_kernel(k_ref, v_ref, state_ref):
    for at in heads_of(k_ref):
        state_ref[at, :] = dot(feature(k_ref[:, at]), v_ref[:, at], TN).astype(BF16)


def local_output_kernel(q_ref, k_ref, v_ref, scores_ref, local_ref):
    keep = causal(q_ref.shape[0])
    for at in heads_of(q_ref):
        scores = dot(feature(q_ref[:, at]), feature(k_ref[:, at]), NT)
        scores = jnp.where(keep, scores, 0.0).astype(BF16)
        scores_ref[:, at] = scores
        local_ref[:, at] = dot(scores, v_ref[:, at], NN)


def grad_output_kernel(q_ref, local_ref, upstream_ref, state_ref, grad_ref, block_ref):
    for at in heads_of(q_ref):
        query = feature(q_ref[:, at])
        output = local_ref[:, at] + dot(query, state_ref[at, :], NN)
        inverse_rms = lax.rsqrt(jnp.mean(output * output, axis=-1, keepdims=True) + EPSILON)
        normed = output * inverse_rms
        upstream = upstream_ref[:, at].astype(F32)
        projection = jnp.mean(upstream * normed, axis=-1, keepdims=True)
        grad = (inverse_rms * (upstream - normed * projection)).astype(BF16)
        grad_ref[:, at] = grad
        block_ref[at, :] = dot(query, grad, TN).astype(BF16)


def local_grads_kernel(
    q_ref, k_ref, v_ref, scores_ref, grad_ref, state_ref, query_out, key_out, value_out
):
    keep = causal(q_ref.shape[0])
    for at in heads_of(q_ref):
        grad = grad_ref[:, at]
        grad_scores = jnp.where(keep, dot(grad, v_ref[:, at], NT), 0.0).astype(BF16)
        query = dot(grad_scores, feature(k_ref[:, at]), NN) + dot(grad, state_ref[at, :], NT)
        query_out[:, at] = (query * slope(q_ref[:, at])).astype(BF16)
        key_out[:, at] = dot(grad_scores, feature(q_ref[:, at]), TN)
        value_out[:, at] = dot(scores_ref[:, at], grad, TN)


def key_grad_kernel(k_ref, v_ref, local_ref, state_ref, key_out, turned_out):
    for at in heads_of(k_ref):
        key = local_ref[:, at] + dot(v_ref[:, at], state_ref[at, :], NT)
        key = key * slope(k_ref[:, at])
        key_out[:, at] = key.astype(BF16)
        turned_out[at, :] = key.T.astype(BF16)


def value_grad_kernel(k_ref, local_ref, state_ref, value_out):
    for at in heads_of(k_ref):
        value_out[:, at] = (local_ref[:, at] + dot(feature(k_ref[:, at]), state_ref[at, :], NN)).astype(
            BF16
        )


def by_heads(kernel, operands, outs, matmuls):
    tokens, features = operands[0][1].shape
    group = 4 * HEAD_DIM
    while features % group:
        group -= HEAD_DIM
    specs = {
        "row": pl.BlockSpec((tokens, group), lambda i: (0, i)),
        "state": pl.BlockSpec((group, HEAD_DIM), lambda i: (i, 0)),
    }
    shapes = {"row": (tokens, features), "state": (features, HEAD_DIM)}
    moved = sum(a.size * a.dtype.itemsize for _, a in operands)
    moved += sum(shapes[kind][0] * shapes[kind][1] * jnp.dtype(dtype).itemsize for kind, dtype in outs)
    return pl.pallas_call(
        kernel,
        grid=(features // group,),
        in_specs=[specs[kind] for kind, _ in operands],
        out_specs=[specs[kind] for kind, _ in outs],
        out_shape=[jax.ShapeDtypeStruct(shapes[kind], dtype) for kind, dtype in outs],
        compiler_params=pltpu.CompilerParams(vmem_limit_bytes=32 * 1024 * 1024),
        cost_estimate=pl.CostEstimate(
            flops=2 * matmuls * tokens * features * HEAD_DIM, bytes_accessed=moved, transcendentals=0
        ),
    )(*[a for _, a in operands])


def swap(array, axis, bit):
    size = lax.axis_size(axis)
    return lax.ppermute(array, axis, [(i, i ^ bit) for i in range(size)])


def shift(array, axis, step):
    size = lax.axis_size(axis)
    return lax.ppermute(array, axis, [(i, i + step) for i in range(size) if 0 <= i + step < size])


def half_of(array, which):
    rows = array.shape[0] // 2
    return lax.dynamic_slice_in_dim(array, which * rows, rows, 0)


def joined(own, other, which):
    return jnp.where(which == 0, jnp.concatenate([own, other]), jnp.concatenate([other, own]))


def add(a, b):
    return (a.astype(F32) + b.astype(F32)).astype(BF16)


def scan_blocks(state, axis, backward):
    place = lax.axis_index(axis)
    core, side = place % 2, (place // 2) % 2
    second = 0 if backward else 1
    sign = -1 if backward else 1
    zero = jnp.zeros((), BF16)

    other = swap(state, axis, 1)
    pair = add(half_of(state, core), half_of(other, core))
    pair_other = swap(pair, axis, 2)
    total = add(half_of(pair, side), half_of(pair_other, side))
    before = None
    running = total
    step = 4
    while step < lax.axis_size(axis):
        arrived = shift(running, axis, sign * step)
        running = add(running, arrived)
        before = arrived if before is None else add(before, arrived)
        step *= 2
    half = joined(before, swap(before, axis, 2), side)
    half = add(half, jnp.where(side == second, pair_other, zero))
    whole = joined(half, swap(half, axis, 1), core)
    return add(whole, jnp.where(core == second, other, zero))


def weight_kernel(which_ref, turned_ref, input_ref, out_ref):
    sources, rows, tokens = turned_ref.shape
    total = jnp.zeros(out_ref.shape, F32)
    for at in range(0, sources, 2):
        pair = jnp.concatenate([turned_ref[at], turned_ref[at + 1]], axis=1)
        total += dot(pair, input_ref[at * tokens : (at + 2) * tokens, :], NN)
    out_ref[...] = total.astype(out_ref.dtype)


def weight_part(turned, inputs, which, parts, dtype):
    sources, rows, tokens = turned.shape
    columns = inputs.shape[1] // parts
    tile = columns
    while tile > 512:
        tile //= 2
    steps = columns // tile
    return pl.pallas_call(
        weight_kernel,
        grid_spec=pltpu.PrefetchScalarGridSpec(
            num_scalar_prefetch=1,
            grid=(steps,),
            in_specs=[
                pl.BlockSpec((sources, rows, tokens), lambda i, which: (0, 0, 0)),
                pl.BlockSpec((sources * tokens, tile), lambda i, which: (0, which[0] * steps + i)),
            ],
            out_specs=pl.BlockSpec((rows, tile), lambda i, which: (0, i)),
        ),
        out_shape=jax.ShapeDtypeStruct((rows, columns), dtype),
        compiler_params=pltpu.CompilerParams(vmem_limit_bytes=40 * 1024 * 1024),
        cost_estimate=pl.CostEstimate(
            flops=2 * sources * tokens * rows * columns,
            bytes_accessed=sources * tokens * columns * 2 + rows * columns * 4,
            transcendentals=0,
        ),
    )(jnp.reshape(which, (1,)).astype(jnp.int32), turned, inputs)


def shards(layer_input, query_rows, key_rows, value_rows, out_grad):
    tokens = query_rows.shape[1]
    query, key, value, upstream = query_rows[0], key_rows[0], value_rows[0], out_grad[0]
    gathered = lax.all_gather(layer_input[0], "ctx", axis=0, tiled=True)

    (block_state,) = by_heads(
        block_state_kernel, [("row", key), ("row", value)], [("state", BF16)], 1
    )
    scores, local_output = by_heads(
        local_output_kernel,
        [("row", query), ("row", key), ("row", value)],
        [("row", BF16), ("row", F32)],
        2,
    )
    state_in = scan_blocks(block_state, "ctx", False)
    grad_output, block_grad = by_heads(
        grad_output_kernel,
        [("row", query), ("row", local_output), ("row", upstream), ("state", state_in)],
        [("row", BF16), ("state", BF16)],
        2,
    )
    query_grad, key_local, value_local = by_heads(
        local_grads_kernel,
        [
            ("row", query),
            ("row", key),
            ("row", value),
            ("row", scores),
            ("row", grad_output),
            ("state", state_in),
        ],
        [("row", BF16), ("row", F32), ("row", F32)],
        5,
    )
    grad_in = scan_blocks(block_grad, "ctx", True)
    key_grad, turned = by_heads(
        key_grad_kernel,
        [("row", key), ("row", value), ("row", key_local), ("state", grad_in)],
        [("row", BF16), ("state", BF16)],
        1,
    )
    (value_grad,) = by_heads(
        value_grad_kernel,
        [("row", key), ("row", value_local), ("state", grad_in)],
        [("row", BF16)],
        1,
    )

    places, parts = lax.axis_size("ctx"), lax.axis_size("dp")
    turned = turned.reshape(places, -1, tokens)
    turned = lax.all_to_all(turned, "ctx", 0, 0)
    scale = (parts * places * tokens) ** (-0.5)
    if parts == 2:
        mine = lax.axis_index("dp")
        sent = weight_part(turned, gathered, 1 - mine, 2, BF16)
        arrived = swap(sent, "dp", 1)
        kept = weight_part(turned, gathered, mine, 2, F32)
        weight_grad = (kept + arrived.astype(F32)) * scale
    else:
        whole = weight_part(turned, gathered, jnp.zeros((), jnp.int32), 1, BF16)
        weight_grad = lax.psum_scatter(whole, "dp", scatter_dimension=1, tiled=True).astype(F32) * scale
    return (query_grad[None], key_grad[None], value_grad[None], weight_grad)


def solution(mesh):
    rows = P("dp", "ctx", None)
    return jax.shard_map(
        shards,
        mesh=mesh,
        in_specs=(rows,) * 5,
        out_specs=(rows, rows, rows, P("ctx", "dp")),
        check_vma=False,
    )
```

```python
import functools

import jax
import jax.numpy as jnp
from jax import lax
from jax.experimental import pallas as pl
from jax.experimental.pallas import tpu as pltpu
from jax.sharding import PartitionSpec as P

HEAD_DIM = 128
EPSILON = 1e-05
F32 = jnp.float32
BF16 = jnp.bfloat16

NN = (((1,), (0,)), ((), ()))
NT = (((1,), (1,)), ((), ()))
TN = (((0,), (0,)), ((), ()))


def dot(a, b, dims):
    return lax.dot_general(a, b, dims, preferred_element_type=F32)


def slope(values):
    wide = values.astype(F32)
    return jnp.where(wide > 0, 1.0, jnp.exp(jnp.minimum(wide, 0.0)))


def feature(values):
    wide = values.astype(F32)
    return jnp.where(wide > 0, wide + 1.0, jnp.exp(jnp.minimum(wide, 0.0))).astype(BF16)


def causal(rows):
    t = lax.broadcasted_iota(jnp.int32, (rows, rows), 0)
    s = lax.broadcasted_iota(jnp.int32, (rows, rows), 1)
    return s <= t


def heads_of(ref):
    for head in range(ref.shape[1] // HEAD_DIM):
        yield slice(head * HEAD_DIM, (head + 1) * HEAD_DIM)


def block_state_kernel(k_ref, v_ref, state_ref):
    for at in heads_of(k_ref):
        state_ref[at, :] = dot(feature(k_ref[:, at]), v_ref[:, at], TN).astype(BF16)


def masked_scores(rows, columns):
    return jnp.where(causal(rows.shape[0]), dot(rows, columns, NT), 0.0).astype(BF16)


def local_output_kernel(q_ref, k_ref, v_ref, local_ref):
    for at in heads_of(q_ref):
        scores = masked_scores(feature(q_ref[:, at]), feature(k_ref[:, at]))
        local_ref[:, at] = dot(scores, v_ref[:, at], NN)


def grad_output_kernel(q_ref, local_ref, upstream_ref, state_ref, grad_ref, block_ref):
    for at in heads_of(q_ref):
        query = feature(q_ref[:, at])
        output = local_ref[:, at] + dot(query, state_ref[at, :], NN)
        inverse_rms = lax.rsqrt(jnp.mean(output * output, axis=-1, keepdims=True) + EPSILON)
        normed = output * inverse_rms
        upstream = upstream_ref[:, at].astype(F32)
        projection = jnp.mean(upstream * normed, axis=-1, keepdims=True)
        grad = (inverse_rms * (upstream - normed * projection)).astype(BF16)
        grad_ref[:, at] = grad
        block_ref[at, :] = dot(query, grad, TN).astype(BF16)


def key_local_kernel(q_ref, v_ref, grad_ref, key_out):
    for at in heads_of(q_ref):
        grad_scores = masked_scores(grad_ref[:, at], v_ref[:, at])
        key_out[:, at] = dot(grad_scores, feature(q_ref[:, at]), TN)


def key_grad_kernel(k_ref, v_ref, local_ref, state_ref, key_out, turned_out):
    for at in heads_of(k_ref):
        key = local_ref[:, at] + dot(v_ref[:, at], state_ref[at, :], NT)
        key = key * slope(k_ref[:, at])
        key_out[:, at] = key.astype(BF16)
        turned = key.T.astype(BF16)
        for copy in range(turned_out.shape[0]):
            turned_out[copy, at, :] = turned


def other_grads_kernel(q_ref, k_ref, v_ref, grad_ref, state_ref, later_ref, query_out, value_out):
    for at in heads_of(k_ref):
        grad = grad_ref[:, at]
        key = feature(k_ref[:, at])
        grad_scores = masked_scores(grad, v_ref[:, at])
        query = dot(grad_scores, key, NN) + dot(grad, state_ref[at, :], NT)
        query_out[:, at] = (query * slope(q_ref[:, at])).astype(BF16)
        scores = masked_scores(feature(q_ref[:, at]), key)
        value = dot(scores, grad, TN) + dot(key, later_ref[at, :], NN)
        value_out[:, at] = value.astype(BF16)


def by_heads(kernel, shape, split, operands, outs, matmuls, into=(), vmem=6):
    tokens, features = shape
    parts, part = split
    width = features // parts
    groups = max(g for g in (1, 2, 3, 4) if width % (g * HEAD_DIM) == 0)
    group = width // groups
    copies = lax.axis_size("dp")
    specs = {
        "row": pl.BlockSpec((tokens, group), lambda i: (0, part * groups + i)),
        "part": pl.BlockSpec((tokens, group), lambda i: (0, i)),
        "state": pl.BlockSpec((group, HEAD_DIM), lambda i: (i, 0)),
        "copies": pl.BlockSpec((copies, group, HEAD_DIM), lambda i: (0, i, 0)),
    }
    shapes = {
        "row": (tokens, features),
        "part": (tokens, width),
        "state": (width, HEAD_DIM),
        "copies": (copies, width, HEAD_DIM),
    }
    moved = tokens * width * 4 * (len(operands) + len(outs))
    held = len(operands)

    def body(*refs):
        kernel(*refs[:held], *refs[held + len(into) :])

    return pl.pallas_call(
        body,
        grid=(groups,),
        in_specs=[specs[kind] for kind, _ in operands] + [pl.BlockSpec(memory_space=pl.ANY)] * len(into),
        out_specs=[specs[kind] for kind, _ in outs],
        out_shape=[jax.ShapeDtypeStruct(shapes[kind], dtype) for kind, dtype in outs],
        input_output_aliases={held + i: i for i in range(len(into))},
        compiler_params=pltpu.CompilerParams(vmem_limit_bytes=vmem * 1024 * 1024),
        cost_estimate=pl.CostEstimate(
            flops=2 * matmuls * tokens * width * HEAD_DIM, bytes_accessed=moved, transcendentals=0
        ),
    )(*[a for _, a in operands], *into)


def swap(array, axis):
    return lax.ppermute(array, axis, [(0, 1), (1, 0)])


def add(a, b):
    return (a.astype(F32) + b.astype(F32)).astype(BF16)


def added_if(flag, a, b):
    return add(a, jnp.where(flag, b, jnp.zeros((), BF16)))


def pick(array, place):
    return jnp.where(place == 0, array[0], array[1])


def both(own, other, place):
    return jnp.where(place == 0, jnp.stack([own, other]), jnp.stack([other, own]))


def after(array, *others):
    if not others:
        return array
    return lax.optimization_barrier((array,) + others)[0]


class Scan:
    def __init__(self, state, bits, backward):
        self.first, self.second, *self.rest = bits
        self.after = 0 if backward else 1
        self.place = {bit: lax.axis_index(bit) for bit in bits}
        self.width = state.shape[0]
        first, second = self.first, self.second
        state = state.reshape(2, 2, self.width // 4, HEAD_DIM)
        self.other = swap(state, first)
        self.pair = add(pick(state, self.place[first]), pick(self.other, self.place[first]))
        self.pair_other = swap(self.pair, second)

    def spread(self, *others):
        place = self.place
        self.pair_other = after(self.pair_other, *others)
        self.total = add(pick(self.pair, place[self.second]), pick(self.pair_other, place[self.second]))
        total, before = self.total, None
        for bit in self.rest:
            arrived = swap(total, bit)
            flag = place[bit] == self.after
            if before is None:
                before = jnp.where(flag, arrived, jnp.zeros((), BF16))
            else:
                before = added_if(flag, before, arrived)
            total = add(total, arrived)
        self.before = before

    def collect(self, *others):
        second, place = self.second, self.place
        before = after(self.before, *others)
        half = both(before, swap(before, second), place[second])
        self.half = added_if(place[second] == self.after, half, self.pair_other)

    def finish(self):
        first, place = self.first, self.place
        whole = both(self.half, swap(self.half, first), place[first])
        whole = added_if(place[first] == self.after, whole, self.other)
        return whole.reshape(self.width, HEAD_DIM)


def sides_kernel(which_ref, in_ref, own_ref, gone_ref):
    columns = own_ref.shape[1]

    @pl.when(which_ref[0] == 0)
    def _():
        own_ref[...] = in_ref[:, :columns]
        gone_ref[...] = in_ref[:, columns:]

    @pl.when(which_ref[0] == 1)
    def _():
        own_ref[...] = in_ref[:, columns:]
        gone_ref[...] = in_ref[:, :columns]


def sides(array, which):
    rows, columns = array.shape
    tile = rows // 4
    out = jax.ShapeDtypeStruct((rows, columns // 2), array.dtype)
    return pl.pallas_call(
        sides_kernel,
        grid_spec=pltpu.PrefetchScalarGridSpec(
            num_scalar_prefetch=1,
            grid=(rows // tile,),
            in_specs=[pl.BlockSpec((tile, columns), lambda i, which: (i, 0))],
            out_specs=[pl.BlockSpec((tile, columns // 2), lambda i, which: (i, 0))] * 2,
        ),
        out_shape=[out, out],
        compiler_params=pltpu.CompilerParams(vmem_limit_bytes=6 * 1024 * 1024),
        cost_estimate=pl.CostEstimate(flops=0, bytes_accessed=4 * array.size, transcendentals=0),
    )(jnp.reshape(which, (1,)).astype(jnp.int32), array)


def weight_kernel(order_ref, turned_ref, *refs):
    *held, kept_ref, sent_ref, lhs_ref = refs
    sources, rows, tokens = turned_ref.shape

    @pl.when(pl.program_id(0) == 0)
    def _():
        for source in range(sources):
            lhs_ref[:, source * tokens : (source + 1) * tokens] = turned_ref[order_ref[source]]

    blocks = [ref[at] for ref in held for at in range(ref.shape[0])]
    total = jnp.zeros(kept_ref.shape, F32)
    for at in range(0, sources, 2):
        lhs = lhs_ref[:, at * tokens : (at + 2) * tokens]
        total += dot(lhs, jnp.concatenate(blocks[at : at + 2], axis=0), NN)
    kept_ref[...] = total
    sent_ref[...] = total.astype(BF16)


def weight_part(order, turned, inputs):
    sources, rows, tokens = turned.shape
    columns = inputs[0].shape[-1]
    tile = 512 if columns % 512 == 0 else columns
    out = pl.BlockSpec((rows, tile), lambda i, order: (0, i))
    return pl.pallas_call(
        weight_kernel,
        grid_spec=pltpu.PrefetchScalarGridSpec(
            num_scalar_prefetch=1,
            grid=(columns // tile,),
            in_specs=[pl.BlockSpec((sources, rows, tokens), lambda i, order: (0, 0, 0))]
            + [pl.BlockSpec((array.shape[0], tokens, tile), lambda i, order: (0, 0, i)) for array in inputs],
            out_specs=[out, out],
            scratch_shapes=[pltpu.VMEM((rows, sources * tokens), BF16)],
        ),
        out_shape=[jax.ShapeDtypeStruct((rows, columns), F32), jax.ShapeDtypeStruct((rows, columns), BF16)],
        compiler_params=pltpu.CompilerParams(vmem_limit_bytes=56 * 1024 * 1024),
        cost_estimate=pl.CostEstimate(
            flops=2 * sources * tokens * rows * columns,
            bytes_accessed=sources * tokens * columns * 2 + rows * columns * 6,
            transcendentals=0,
        ),
    )(order, turned, *inputs)


def shards(layer_input, query_rows, key_rows, value_rows, out_grad, bits):
    query, key, value, upstream = query_rows[0], key_rows[0], value_rows[0], out_grad[0]
    shape = tokens, features = query.shape
    sequences = lax.axis_size("dp")
    places = 2 ** len(bits)
    core, side, layer, *high = bits
    spans = tuple(reversed(high))
    halves = places // 8
    rows = features // places

    def run(kernel, part, operands, outs, matmuls, into=()):
        return by_heads(kernel, shape, (halves, part), operands, outs, matmuls, into)

    mine = lax.axis_index("dp")
    if sequences == 2:
        own, gone = sides(layer_input[0], mine)
        held = [own[None], swap(gone, "dp")[None]]
        order = jnp.arange(2, dtype=jnp.int32) ^ mine
    else:
        held = [lax.all_to_all(layer_input[0].reshape(tokens, sequences, -1), "dp", 1, 0)]
        order = jnp.arange(sequences, dtype=jnp.int32)
    order = order * 8

    parts = range(halves)
    forward, backward, outputs, states, grads, key_locals, turns = [], [], [], [], [], [], []
    for part in parts:
        (block_state,) = run(block_state_kernel, part, [("row", key), ("row", value)], [("state", BF16)], 1)
        forward.append(Scan(block_state, bits, False))
    pairs = [scan.pair for scan in forward]

    def spread_inputs(held, order, bit, weight, *others):
        at = lax.axis_index(bit) * weight
        held = held + [swap(after(array, *others), bit) for array in held]
        return held, jnp.concatenate([order + at, order + weight - at])

    near, order = spread_inputs(held, order, side, 2, *pairs)

    for part in parts:
        outputs += run(
            local_output_kernel,
            part,
            [("row", after(query, *pairs)), ("row", key), ("row", value)],
            [("part", F32)],
            2,
        )
    for part in parts:
        forward[part].spread(*outputs, *held)
    arrived = [scan.before for scan in forward]
    for part in parts:
        forward[part].collect(*near)
    held, order = spread_inputs(near, order, layer, 4, *arrived)
    for part in parts:
        states.append(forward[part].finish())
        grad_output, block_grad = run(
            grad_output_kernel,
            part,
            [("row", query), ("part", outputs[part]), ("row", upstream), ("state", states[part])],
            [("part", BF16), ("state", BF16)],
            2,
        )
        grads.append(grad_output)
        backward.append(Scan(block_grad, bits, True))
    pairs = [scan.pair for scan in backward]
    for part in parts:
        key_locals += run(
            key_local_kernel,
            part,
            [("row", query), ("row", value), ("part", after(grads[part], *pairs))],
            [("part", F32)],
            2,
        )
    for part in parts:
        backward[part].spread(*key_locals)
    for part in parts:
        backward[part].collect(*held)
    halves_in = [scan.half for scan in backward]
    held, order = spread_inputs(held, order, core, 1)

    key_grad, other_grads = [], []
    for part in parts:
        later = backward[part].finish()
        *key_grad, turned = run(
            key_grad_kernel,
            part,
            [("row", key), ("row", value), ("part", key_locals[part]), ("state", later)],
            [("row", BF16), ("copies", BF16)],
            1,
            key_grad,
        )
        turns.append(after(turned, *halves_in))
        other_grads = run(
            other_grads_kernel,
            part,
            [
                ("row", query),
                ("row", key),
                ("row", value),
                ("part", after(grads[part], *turns)),
                ("state", states[part]),
                ("state", later),
            ],
            [("row", BF16), ("row", BF16)],
            6,
            other_grads,
        )
    query_grad, value_grad = other_grads

    span = lax.axis_index(spans)
    weight_grad = None
    for target, turned in enumerate(turns):
        turned = turned.reshape(sequences * 8, rows, tokens)
        turned = lax.all_to_all(turned, ("dp", layer, side, core), 0, 0, tiled=True)
        kept, sent = weight_part(order, turned, held)
        for turn in range(1, halves):
            kept += lax.ppermute(sent, spans, [((target + turn) % halves, target)]).astype(F32)
        weight_grad = kept if weight_grad is None else jnp.where(span == target, kept, weight_grad)
    weight_grad = weight_grad * (sequences * places * tokens) ** (-0.5)
    return (query_grad[None], key_grad[0][None], value_grad[None], weight_grad)


def solution(mesh):
    sequences, places = mesh.shape["dp"], mesh.shape["ctx"]
    bits = tuple(f"bit{i}" for i in range(places.bit_length() - 1))
    ctx = tuple(reversed(bits))
    devices = mesh.devices.reshape((sequences,) + (2,) * len(bits))
    rows = P("dp", ctx, None)
    return jax.shard_map(
        functools.partial(shards, bits=bits),
        mesh=jax.sharding.Mesh(devices, ("dp",) + ctx),
        in_specs=(rows,) * 5,
        out_specs=(rows, rows, rows, P(ctx, "dp")),
        check_vma=False,
    )
```

```python
import functools

import jax
import jax.numpy as jnp
from jax import lax
from jax.experimental import pallas as pl
from jax.experimental.pallas import tpu as pltpu
from jax.sharding import PartitionSpec as P

HEAD_DIM = 128
EPSILON = 1e-05
VMEM_MIB = 56
F32 = jnp.float32
BF16 = jnp.bfloat16

NN = (((1,), (0,)), ((), ()))
NT = (((1,), (1,)), ((), ()))
TN = (((0,), (0,)), ((), ()))


def dot(a, b, dims):
    return lax.dot_general(a, b, dims, preferred_element_type=F32)


def slope(values):
    wide = values.astype(F32)
    return jnp.where(wide > 0, 1.0, jnp.exp(jnp.minimum(wide, 0.0)))


def feature(values):
    wide = values.astype(F32)
    return jnp.where(wide > 0, wide + 1.0, jnp.exp(jnp.minimum(wide, 0.0))).astype(BF16)


def causal_scores(rows, columns):
    scores = dot(rows, columns, NT)
    t = lax.broadcasted_iota(jnp.int32, scores.shape, 0)
    s = lax.broadcasted_iota(jnp.int32, scores.shape, 1)
    return jnp.where(s <= t, scores, 0.0).astype(BF16)


def causal_scores_turned(rows, columns):
    scores = dot(columns, rows, NT)
    s = lax.broadcasted_iota(jnp.int32, scores.shape, 0)
    t = lax.broadcasted_iota(jnp.int32, scores.shape, 1)
    return jnp.where(s <= t, scores, 0.0).astype(BF16)


def block_state_head(at, k_ref, v_ref, state_ref):
    state_ref[at, :] = dot(feature(k_ref[:, at]), v_ref[:, at], TN).astype(BF16)


def local_output_head(at, q_ref, k_ref, v_ref, local_ref):
    scores = causal_scores(feature(q_ref[:, at]), feature(k_ref[:, at]))
    local_ref[:, at] = dot(scores, v_ref[:, at], NN)


def assemble(at, flags_ref, other_ref, quarter_refs, state_ref):
    size = quarter_refs[0].shape[0]
    quarter, start = divmod(at.start, size)
    near = flags_ref[0] == quarter // 2
    same = flags_ref[1] == quarter % 2
    own, other, swapped_own, swapped_other = [ref[start : start + HEAD_DIM, :] for ref in quarter_refs]
    total = jnp.where(same, jnp.where(near, own, swapped_own), jnp.where(near, other, swapped_other))
    total = added_if(flags_ref[2] == 1, total, other_ref[at, :])
    state_ref[at, :] = total
    return total


def grad_output_head(at, flags_ref, q_ref, local_ref, upstream_ref, other_ref, *refs):
    *quarter_refs, grad_ref, block_ref, state_ref = refs
    state = assemble(at, flags_ref, other_ref, quarter_refs, state_ref)
    query = feature(q_ref[:, at])
    output = local_ref[:, at] + dot(query, state, NN)
    inverse_rms = lax.rsqrt(jnp.mean(output * output, axis=-1, keepdims=True) + EPSILON)
    normed = output * inverse_rms
    upstream = upstream_ref[:, at].astype(F32)
    projection = jnp.mean(upstream * normed, axis=-1, keepdims=True)
    grad = (inverse_rms * (upstream - normed * projection)).astype(BF16)
    grad_ref[:, at] = grad
    block_ref[at, :] = dot(query, grad, TN).astype(BF16)


def key_local_head(at, q_ref, v_ref, grad_ref, key_out):
    grad_scores = causal_scores_turned(grad_ref[:, at], v_ref[:, at])
    key_out[:, at] = dot(grad_scores, feature(q_ref[:, at]), NN)


def key_grad_head(at, flags_ref, k_ref, v_ref, local_ref, other_ref, *refs):
    *quarter_refs, key_out, turned_out, state_ref = refs
    cuts, copies, devices, halves, rows, tokens = turned_out.shape
    state = assemble(at, flags_ref, other_ref, quarter_refs, state_ref)
    key = local_ref[:, at] + dot(v_ref[:, at], state, NT)
    key = (key * slope(k_ref[:, at])).astype(BF16)
    key_out[:, at] = key
    turned = key.T
    start = at.start
    while start < at.stop:
        block, row = divmod(start, rows)
        size = min(rows - row, at.stop - start)
        owner, cut = divmod(block, cuts)
        half, device = divmod(owner, devices)
        for copy in range(copies):
            turned_out[cut, copy, device, half, row : row + size] = turned[start - at.start : start - at.start + size]
        start += size


def other_grads_head(at, q_ref, k_ref, v_ref, grad_ref, state_ref, later_ref, query_out, value_out):
    grad = grad_ref[:, at]
    key = feature(k_ref[:, at])
    grad_scores = causal_scores(grad, v_ref[:, at])
    query = dot(grad_scores, key, NN) + dot(grad, state_ref[at, :], NT)
    query_out[:, at] = (query * slope(q_ref[:, at])).astype(BF16)
    scores = causal_scores_turned(feature(q_ref[:, at]), key)
    value = dot(scores, grad, NN) + dot(key, later_ref[at, :], NN)
    value_out[:, at] = value.astype(BF16)


def by_heads(head, operands, outs, matmuls, flags=None, vmem=12):
    tokens, features = operands[0][1].shape
    groups = 2 if features % (2 * HEAD_DIM) == 0 else 1
    group = features // groups
    shapes = {"row": (tokens, features), "state": (features, HEAD_DIM)}
    shapes_held = {"held row": shapes["row"], "held state": shapes["state"]}
    kinds = [kind for kind, _ in operands] + [kind for kind, _ in outs]
    results = [
        jax.ShapeDtypeStruct(shapes.get(kind) or shapes_held.get(kind, kind), dtype) for kind, dtype in outs
    ]
    held = [kind == "held" or kind in shapes_held for kind in kinds]
    arrays = [array for _, array in operands] + results
    count = len(operands)

    def part(kind, ref, index):
        cut = pl.ds(index * group, group)
        return ref.at[:, cut] if kind == "row" else ref.at[cut, :]

    def body(*refs):
        numbers = [] if flags is None else [refs[0]]
        refs = refs[len(numbers) :]
        there, moved = refs[: len(kinds)], refs[-1]
        scratch = iter(refs[len(kinds) : -1])
        here = [ref if stays else next(scratch) for stays, ref in zip(held, there)]

        def copy(index, step):
            source, target = (there, here) if index < count else (here, there)
            source, target = source[index], target[index]
            if kinds[index] in shapes:
                source, target = part(kinds[index], source, step), part(kinds[index], target, step)
            return pltpu.make_async_copy(source, target, moved.at[index, step])

        def at_once(index, step):
            return step == (0 if index < count else groups - 1)

        def due(step, indices):
            moving = [index for index in indices if not held[index]]
            return [index for index in moving if kinds[index] in shapes or at_once(index, step)]

        ins, outputs = range(count), range(count, len(kinds))
        for step in range(groups):
            for index in due(step, ins):
                copy(index, step).start()
        for step in range(groups):
            for index in due(step, ins):
                copy(index, step).wait()
            for start in range(step * group, (step + 1) * group, HEAD_DIM):
                head(slice(start, start + HEAD_DIM), *numbers, *here)
            for index in due(step, outputs):
                copy(index, step).start()
        for step in range(groups):
            for index in due(step, outputs):
                copy(index, step).wait()

    anywhere = pl.BlockSpec(memory_space=pl.ANY)
    places = [pl.BlockSpec(memory_space=pltpu.VMEM) if stays else anywhere for stays in held]
    return pl.pallas_call(
        body,
        in_specs=([] if flags is None else [pl.BlockSpec(memory_space=pltpu.SMEM)]) + places[:count],
        out_specs=places[count:],
        out_shape=results,
        scratch_shapes=[
            pltpu.VMEM(array.shape, array.dtype) for stays, array in zip(held, arrays) if not stays
        ]
        + [pltpu.SemaphoreType.DMA((len(kinds), groups))],
        compiler_params=pltpu.CompilerParams(vmem_limit_bytes=vmem * 1024 * 1024),
        cost_estimate=pl.CostEstimate(
            flops=2 * matmuls * tokens * features * HEAD_DIM,
            bytes_accessed=tokens * features * 2 * len(kinds),
            transcendentals=0,
        ),
    )(*([] if flags is None else [flags]), *[array for _, array in operands])


def swap(array, axis):
    return lax.ppermute(array, axis, [(0, 1), (1, 0)])


def added_if(flag, a, b):
    return (a.astype(F32) + jnp.where(flag, b.astype(F32), 0.0)).astype(BF16)


def small(body, flags, arrays, outs):
    vmem = pl.BlockSpec(memory_space=pltpu.VMEM)
    result = jax.ShapeDtypeStruct(arrays[-1].shape[-2:], BF16)

    def kernel(*refs):
        values = body(*refs[: 1 + len(arrays)])
        for ref, value in zip(refs[1 + len(arrays) :], values):
            ref[...] = value

    return pl.pallas_call(
        kernel,
        in_specs=[pl.BlockSpec(memory_space=pltpu.SMEM)] + [vmem] * len(arrays),
        out_specs=[vmem] * outs,
        out_shape=[result] * outs,
        compiler_params=pltpu.CompilerParams(vmem_limit_bytes=4 * 1024 * 1024),
        cost_estimate=pl.CostEstimate(flops=0, bytes_accessed=1024, transcendentals=0),
    )(flags, *arrays)


def after(array, *others):
    if not others:
        return array
    return lax.optimization_barrier((array,) + others)[0]


class Scan:
    def __init__(self, state, bits, backward):
        first, second, *self.rest = bits
        self.first, self.second = first, second
        after = 0 if backward else 1
        place = [lax.axis_index(bit) for bit in bits]
        self.flags = jnp.stack([*place, *[(at == after).astype(jnp.int32) for at in place]])
        self.counts = len(bits)
        state = state.reshape(2, 2, -1, HEAD_DIM)
        self.other = swap(state, first)

        def quarters(flags, state, other):
            core, side = flags[0], flags[1]
            return [added_if(True, state[core, at], other[core, at]) for at in (1 - side, side)]

        self.theirs, self.mine = small(quarters, self.flags, [state, self.other], 2)
        self.arrived = swap(self.theirs, second)

    def spread(self, due, meanwhile):
        counts = self.counts
        self.arrived = after(self.arrived, *due)

        def start(flags, mine, arrived):
            return [added_if(True, mine[...], arrived[...])]

        (total,) = small(start, self.flags, [self.mine, self.arrived], 1)
        self.rest_arrived = swap(after(self.mine, self.arrived), self.second)
        before = None
        for index, bit in enumerate(self.rest, 2):
            last = bit == self.rest[-1]
            pieces = meanwhile(total) if last else [self.rest_arrived]
            arrived = after(swap(total, bit), *pieces)

            def first(flags, total, arrived):
                values = arrived[...], total[...]
                return [jnp.where(flags[counts + 2] == 1, values[0], 0.0), added_if(True, *values)]

            def middle(flags, total, arrived, before):
                value = added_if(flags[counts + index] == 1, before[...], arrived[...])
                return [value, added_if(True, total[...], arrived[...])]

            def final(flags, side, arrived, before):
                value = added_if(flags[counts + index] == 1, before[...], arrived[...])
                return [value, added_if(flags[counts + 1] == 1, value, side[...])]

            if before is None:
                before, total = small(first, self.flags, [total, arrived], 2)
            elif not last:
                before, total = small(middle, self.flags, [total, arrived, before], 2)
            else:
                self.before, self.own = small(final, self.flags, [self.arrived, arrived, before], 2)

    def collect(self):
        counts = self.counts

        def finish(flags, swapped, rest):
            return [added_if(flags[counts + 1] == 1, swapped[...], rest[...])]

        arrays = [swap(self.before, self.second), self.rest_arrived]
        (other,) = small(finish, self.flags, arrays, 1)
        quarters = [self.own, other, swap(self.own, self.first), swap(other, self.first)]
        self.kinds = jnp.stack([self.flags[0], self.flags[1], self.flags[counts]])
        self.operands = [("whole", self.other.reshape(-1, HEAD_DIM))]
        self.operands += [("held", quarter) for quarter in quarters]


def sides_kernel(which_ref, in_ref, own_ref, gone_ref):
    columns = own_ref.shape[1]

    @pl.when(which_ref[0] == 0)
    def _():
        own_ref[...] = in_ref[:, :columns]
        gone_ref[...] = in_ref[:, columns:]

    @pl.when(which_ref[0] == 1)
    def _():
        own_ref[...] = in_ref[:, columns:]
        gone_ref[...] = in_ref[:, :columns]


def sides(array, which):
    rows, columns = array.shape
    tile = rows // 4
    out = jax.ShapeDtypeStruct((rows, columns // 2), array.dtype)
    return pl.pallas_call(
        sides_kernel,
        grid_spec=pltpu.PrefetchScalarGridSpec(
            num_scalar_prefetch=1,
            grid=(rows // tile,),
            in_specs=[pl.BlockSpec((tile, columns), lambda i, which: (i, 0))],
            out_specs=[pl.BlockSpec((tile, columns // 2), lambda i, which: (i, 0))] * 2,
        ),
        out_shape=[out, out],
        compiler_params=pltpu.CompilerParams(vmem_limit_bytes=6 * 1024 * 1024),
        cost_estimate=pl.CostEstimate(flops=0, bytes_accessed=4 * array.size, transcendentals=0),
    )(jnp.reshape(which, (1,)).astype(jnp.int32), array)


def weight_kernel(order_ref, turned_ref, *refs):
    *held, kept_ref, sent_ref, total_ref, buffer_ref, arrival = refs
    sources, _, tokens = turned_ref.shape
    others, rows, columns = sent_ref.shape
    copies, at = [], 0
    for index, ref in enumerate(held):
        count = ref.shape[0]
        copies.append(pltpu.make_async_copy(ref, buffer_ref.at[at : at + count], arrival.at[index]))
        copies[-1].start()
        at += count
    per_step, tile = 4, 512 if columns % 512 == 0 else columns
    steps = sources // per_step
    for step in range(steps):
        for copy in copies[step * len(copies) // steps : (step + 1) * len(copies) // steps]:
            copy.wait()
        first = step * per_step
        lhs = jnp.concatenate([turned_ref[order_ref[first + i]] for i in range(per_step)], axis=1)
        for start in range(0, columns, tile):
            cut = slice(start, start + tile)
            rhs = buffer_ref[first : first + per_step, :, cut].reshape(per_step * tokens, tile)
            product = dot(lhs, rhs, NN)
            total_ref[:, cut] = product if step == 0 else total_ref[:, cut] + product
    span = order_ref[sources]
    kept_ref[...] = total_ref[pl.ds(pl.multiple_of(span * rows, 16), rows), :]
    for turn in range(others):
        target = lax.rem(span + turn + 1, others + 1)
        sent_ref[turn] = total_ref[pl.ds(pl.multiple_of(target * rows, 16), rows), :].astype(BF16)


def weight_part(order, turned, inputs, halves):
    sources, rows, tokens = turned.shape
    columns = inputs[0].shape[-1]
    vmem = pl.BlockSpec(memory_space=pltpu.VMEM)
    return pl.pallas_call(
        weight_kernel,
        in_specs=[pl.BlockSpec(memory_space=pltpu.SMEM), vmem]
        + [pl.BlockSpec(memory_space=pl.ANY)] * len(inputs),
        out_specs=[vmem, vmem],
        out_shape=[
            jax.ShapeDtypeStruct((rows // halves, columns), F32),
            jax.ShapeDtypeStruct((halves - 1, rows // halves, columns), BF16),
        ],
        scratch_shapes=[
            pltpu.VMEM((rows, columns), F32),
            pltpu.VMEM((sources, tokens, columns), BF16),
            pltpu.SemaphoreType.DMA((len(inputs),)),
        ],
        compiler_params=pltpu.CompilerParams(vmem_limit_bytes=VMEM_MIB * 1024 * 1024),
        cost_estimate=pl.CostEstimate(
            flops=2 * sources * tokens * rows * columns,
            bytes_accessed=sources * tokens * columns * 2 + rows * columns * 6,
            transcendentals=0,
        ),
    )(order, turned, *inputs)


def shards(layer_input, query_rows, key_rows, value_rows, out_grad, bits):
    query, key, value, upstream = query_rows[0], key_rows[0], value_rows[0], out_grad[0]
    tokens, features = query.shape
    sequences = lax.axis_size("dp")
    places = 2 ** len(bits)
    core, side, layer, *high = bits
    spans = tuple(reversed(high))
    halves = places // 8
    cuts = 2
    rows = features // places // cuts

    mine = lax.axis_index("dp")
    if sequences == 2:
        own, gone = sides(layer_input[0], mine)
        own, far = own[None], swap(gone, "dp")[None]
        own_id, far_id = mine[None], 1 - mine[None]
    else:
        wide = lax.all_to_all(layer_input[0].reshape(tokens, sequences, -1), "dp", 1, 0)
        own, far = wide[: sequences // 2], wide[sequences // 2 :]
        own_id, far_id = jnp.split(jnp.arange(sequences), 2)
    own_layer = swap(own, layer)

    (block_state,) = by_heads(block_state_head, [("row", key), ("row", value)], [("held state", BF16)], 1)
    forward = Scan(block_state, bits, False)
    (output,) = by_heads(
        local_output_head,
        [("held", after(query, forward.mine)), ("held", key), ("held", value)],
        [("held row", F32)],
        2,
    )
    far_side = []

    def along_side(token):
        far_side.append(swap(after(far, token), side))
        return far_side

    forward.spread([output, far, own_layer], along_side)
    forward.collect()
    far_layer = swap(after(far, forward.before), layer)
    grad_output, block_grad, state_in = by_heads(
        grad_output_head,
        [("held", query), ("held", output), ("held", upstream), *forward.operands],
        [("held row", BF16), ("held state", BF16), ("state", BF16)],
        2,
        after(forward.kinds, far_layer),
    )
    backward = Scan(block_grad, bits, True)
    (key_local,) = by_heads(
        key_local_head,
        [("held", query), ("held", value), ("held", after(grad_output, backward.mine))],
        [("held row", F32)],
        2,
    )
    far_both = swap(after(far_side[0], backward.mine), layer)
    own_side = []

    def along_side_again(token):
        own_side.append(swap(after(own, token), side))
        return own_side

    backward.spread([key_local, far_both], along_side_again)
    backward.collect()
    own_both = swap(after(own_side[0], backward.before), layer)
    key_grad, turned, grad_in = by_heads(
        key_grad_head,
        [("held", key), ("held", value), ("held", key_local), *backward.operands],
        [("row", BF16), ((cuts, sequences, 8, halves, rows, tokens), BF16), ("state", BF16)],
        1,
        backward.kinds,
    )
    turned = after(turned, own_both)
    held, order = [], []
    for array, ids, layered, sided in (
        (own, own_id, 0, 0),
        (far, far_id, 0, 0),
        (own_layer, own_id, 1, 0),
        (far_layer, far_id, 1, 0),
        (far_side[0], far_id, 0, 1),
        (far_both, far_id, 1, 1),
        (own_side[0], own_id, 0, 1),
        (own_both, own_id, 1, 1),
    ):
        held.append(array)
        order.append(8 * ids + 4 * (lax.axis_index(layer) ^ layered) + 2 * (lax.axis_index(side) ^ sided))
    held += [swap(array, core) for array in held]
    at = lax.axis_index(core)
    span = lax.axis_index(spans)
    order = jnp.concatenate([ids + at for ids in order] + [ids + 1 - at for ids in order] + [span[None]])
    order = order.astype(jnp.int32)

    sums, done = [], turned
    for cut in range(cuts):
        part = turned[cut].reshape(sequences * 8, halves * rows, tokens)
        part = lax.all_to_all(part, ("dp", layer, side, core), 0, 0, tiled=True)
        total, sent = weight_part(order, after(part, done), held, halves)
        for turn in range(1, halves):
            moved = lax.ppermute(sent[turn - 1], spans, [(i, (i + turn) % halves) for i in range(halves)])
            total += moved.astype(F32)
        done = sent
        sums.append(total)
    weight_grad = jnp.concatenate(sums) * (sequences * places * tokens) ** (-0.5)
    query_grad, value_grad = by_heads(
        other_grads_head,
        [
            ("held", query),
            ("held", key),
            ("held", value),
            ("held", after(grad_output, done)),
            ("state", state_in),
            ("state", grad_in),
        ],
        [("row", BF16), ("row", BF16)],
        6,
    )
    return (query_grad[None], key_grad[None], value_grad[None], weight_grad)


def solution(mesh):
    sequences, places = mesh.shape["dp"], mesh.shape["ctx"]
    bits = tuple(f"bit{i}" for i in range(places.bit_length() - 1))
    ctx = tuple(reversed(bits))
    devices = mesh.devices.reshape((sequences,) + (2,) * len(bits))
    rows = P("dp", ctx, None)
    return jax.shard_map(
        functools.partial(shards, bits=bits),
        mesh=jax.sharding.Mesh(devices, ("dp",) + ctx),
        in_specs=(rows,) * 5,
        out_specs=(rows, rows, rows, P(ctx, "dp")),
        check_vma=False,
    )
```

```python
import functools

import jax
import jax.numpy as jnp
from jax import lax
from jax.experimental import pallas as pl
from jax.experimental.pallas import tpu as pltpu
from jax.sharding import PartitionSpec as P

HEAD_DIM = 128
EPSILON = 1e-05
VMEM_MIB = 56
F32 = jnp.float32
BF16 = jnp.bfloat16

NN = (((1,), (0,)), ((), ()))
NT = (((1,), (1,)), ((), ()))
TN = (((0,), (0,)), ((), ()))


def dot(a, b, dims):
    return lax.dot_general(a, b, dims, preferred_element_type=F32)


def slope(values):
    wide = values.astype(F32)
    return jnp.where(wide > 0, 1.0, jnp.exp(jnp.minimum(wide, 0.0)))


def feature(values):
    wide = values.astype(F32)
    return jnp.where(wide > 0, wide + 1.0, jnp.exp(jnp.minimum(wide, 0.0))).astype(BF16)


def causal_scores(rows, columns):
    scores = dot(rows, columns, NT)
    t = lax.broadcasted_iota(jnp.int32, scores.shape, 0)
    s = lax.broadcasted_iota(jnp.int32, scores.shape, 1)
    return jnp.where(s <= t, scores, 0.0).astype(BF16)


def causal_scores_turned(rows, columns):
    scores = dot(columns, rows, NT)
    s = lax.broadcasted_iota(jnp.int32, scores.shape, 0)
    t = lax.broadcasted_iota(jnp.int32, scores.shape, 1)
    return jnp.where(s <= t, scores, 0.0).astype(BF16)


def block_state_head(at, k_ref, v_ref, state_ref):
    state_ref[at, :] = dot(feature(k_ref[:, at]), v_ref[:, at], TN).astype(BF16)


def local_output_head(at, q_ref, k_ref, v_ref, local_ref):
    scores = causal_scores(feature(q_ref[:, at]), feature(k_ref[:, at]))
    local_ref[:, at] = dot(scores, v_ref[:, at], NN)


def assemble(at, counts, flags_ref, other_ref, quarter_refs, state_ref):
    size = quarter_refs[0].shape[0]
    quarter, start = divmod(at.start, size)
    near = flags_ref[0] == quarter // 2
    same = flags_ref[1] == quarter % 2
    own, other, swapped_own, swapped_other = [ref[start : start + HEAD_DIM, :] for ref in quarter_refs]
    total = jnp.where(same, jnp.where(near, own, swapped_own), jnp.where(near, other, swapped_other))
    total = added_if(flags_ref[counts] == 1, total, other_ref[at, :])
    state_ref[at, :] = total
    return total


def grad_output_head(counts, at, flags_ref, q_ref, local_ref, upstream_ref, other_ref, *refs):
    *quarter_refs, grad_ref, block_ref, state_ref = refs
    state = assemble(at, counts, flags_ref, other_ref, quarter_refs, state_ref)
    query = feature(q_ref[:, at])
    output = local_ref[:, at] + dot(query, state, NN)
    inverse_rms = lax.rsqrt(jnp.mean(output * output, axis=-1, keepdims=True) + EPSILON)
    normed = output * inverse_rms
    upstream = upstream_ref[:, at].astype(F32)
    projection = jnp.mean(upstream * normed, axis=-1, keepdims=True)
    grad = (inverse_rms * (upstream - normed * projection)).astype(BF16)
    grad_ref[:, at] = grad
    block_ref[at, :] = dot(query, grad, TN).astype(BF16)


def key_local_head(at, q_ref, v_ref, grad_ref, key_out):
    grad_scores = causal_scores_turned(grad_ref[:, at], v_ref[:, at])
    key_out[:, at] = dot(grad_scores, feature(q_ref[:, at]), NN)


def key_grad_head(counts, at, flags_ref, k_ref, v_ref, local_ref, other_ref, *refs):
    *quarter_refs, key_out, state_ref = refs[:6]
    turned_out = refs[6:]
    cuts = len(turned_out)
    copies, devices, halves, rows, tokens = turned_out[0].shape
    state = assemble(at, counts, flags_ref, other_ref, quarter_refs, state_ref)
    key = local_ref[:, at] + dot(v_ref[:, at], state, NT)
    key = (key * slope(k_ref[:, at])).astype(BF16)
    key_out[:, at] = key
    turned = key.T
    start = at.start
    while start < at.stop:
        block, row = divmod(start, rows)
        size = min(rows - row, at.stop - start)
        owner, cut = divmod(block, cuts)
        half, device = divmod(owner, devices)
        for copy in range(copies):
            turned_out[cut][copy, device, half, row : row + size] = turned[start - at.start : start - at.start + size]
        start += size


def other_grads_head(at, q_ref, k_ref, v_ref, grad_ref, state_ref, later_ref, query_out, value_out):
    grad = grad_ref[:, at]
    key = feature(k_ref[:, at])
    grad_scores = causal_scores(grad, v_ref[:, at])
    query = dot(grad_scores, key, NN) + dot(grad, state_ref[at, :], NT)
    query_out[:, at] = (query * slope(q_ref[:, at])).astype(BF16)
    scores = causal_scores_turned(feature(q_ref[:, at]), key)
    value = dot(scores, grad, NN) + dot(key, later_ref[at, :], NN)
    value_out[:, at] = value.astype(BF16)


def by_heads(head, operands, outs, matmuls, flags=None, vmem=12):
    tokens, features = operands[0][1].shape
    groups = 2 if features % (2 * HEAD_DIM) == 0 else 1
    group = features // groups
    shapes = {"row": (tokens, features), "state": (features, HEAD_DIM)}
    shapes_held = {"held row": shapes["row"], "held state": shapes["state"]}
    kinds = [kind for kind, _ in operands] + [kind for kind, _ in outs]
    results = [
        jax.ShapeDtypeStruct(shapes.get(kind) or shapes_held.get(kind, kind), dtype) for kind, dtype in outs
    ]
    held = [kind == "held" or kind in shapes_held for kind in kinds]
    arrays = [array for _, array in operands] + results
    count = len(operands)

    def part(kind, ref, index):
        cut = pl.ds(index * group, group)
        return ref.at[:, cut] if kind == "row" else ref.at[cut, :]

    def body(*refs):
        numbers = [] if flags is None else [refs[0]]
        refs = refs[len(numbers) :]
        there, moved = refs[: len(kinds)], refs[-1]
        scratch = iter(refs[len(kinds) : -1])
        here = [ref if stays else next(scratch) for stays, ref in zip(held, there)]

        def copy(index, step):
            source, target = (there, here) if index < count else (here, there)
            source, target = source[index], target[index]
            if kinds[index] in shapes:
                source, target = part(kinds[index], source, step), part(kinds[index], target, step)
            return pltpu.make_async_copy(source, target, moved.at[index, step])

        def at_once(index, step):
            return step == (0 if index < count else groups - 1)

        def due(step, indices):
            moving = [index for index in indices if not held[index]]
            return [index for index in moving if kinds[index] in shapes or at_once(index, step)]

        ins, outputs = range(count), range(count, len(kinds))
        for step in range(groups):
            for index in due(step, ins):
                copy(index, step).start()
        for step in range(groups):
            for index in due(step, ins):
                copy(index, step).wait()
            for start in range(step * group, (step + 1) * group, HEAD_DIM):
                head(slice(start, start + HEAD_DIM), *numbers, *here)
            for index in due(step, outputs):
                copy(index, step).start()
        for step in range(groups):
            for index in due(step, outputs):
                copy(index, step).wait()

    anywhere = pl.BlockSpec(memory_space=pl.ANY)
    places = [pl.BlockSpec(memory_space=pltpu.VMEM) if stays else anywhere for stays in held]
    return pl.pallas_call(
        body,
        in_specs=([] if flags is None else [pl.BlockSpec(memory_space=pltpu.SMEM)]) + places[:count],
        out_specs=places[count:],
        out_shape=results,
        scratch_shapes=[
            pltpu.VMEM(array.shape, array.dtype) for stays, array in zip(held, arrays) if not stays
        ]
        + [pltpu.SemaphoreType.DMA((len(kinds), groups))],
        compiler_params=pltpu.CompilerParams(vmem_limit_bytes=vmem * 1024 * 1024),
        cost_estimate=pl.CostEstimate(
            flops=2 * matmuls * tokens * features * HEAD_DIM,
            bytes_accessed=tokens * features * 2 * len(kinds),
            transcendentals=0,
        ),
    )(*([] if flags is None else [flags]), *[array for _, array in operands])


def swap(array, axis):
    return lax.ppermute(array, axis, [(0, 1), (1, 0)])


def added_if(flag, a, b):
    return (a.astype(F32) + jnp.where(flag, b.astype(F32), 0.0)).astype(BF16)


def small(body, flags, arrays, outs):
    vmem = pl.BlockSpec(memory_space=pltpu.VMEM)
    result = jax.ShapeDtypeStruct(arrays[-1].shape[-2:], BF16)

    def kernel(*refs):
        values = body(*refs[: 1 + len(arrays)])
        for ref, value in zip(refs[1 + len(arrays) :], values):
            ref[...] = value

    return pl.pallas_call(
        kernel,
        in_specs=[pl.BlockSpec(memory_space=pltpu.SMEM)] + [vmem] * len(arrays),
        out_specs=[vmem] * outs,
        out_shape=[result] * outs,
        compiler_params=pltpu.CompilerParams(vmem_limit_bytes=4 * 1024 * 1024),
        cost_estimate=pl.CostEstimate(flops=0, bytes_accessed=1024, transcendentals=0),
    )(flags, *arrays)


def after(array, *others):
    if not others:
        return array
    return lax.optimization_barrier((array,) + others)[0]


class Scan:
    def __init__(self, state, bits, backward, flags):
        first, second, *self.rest = bits
        self.first, self.second = first, second
        self.flags, self.counts = flags, (2 if backward else 1) * len(bits)
        state = state.reshape(2, 2, -1, HEAD_DIM)
        self.other = swap(state, first)

        def quarters(flags, state, other):
            core, side = flags[0], flags[1]
            return [added_if(True, state[core, at], other[core, at]) for at in (1 - side, side)]

        self.theirs, self.mine = small(quarters, self.flags, [state, self.other], 2)
        self.arrived = swap(self.theirs, second)

    def spread(self, due, early, meanwhile, rest_early):
        counts = self.counts
        self.arrived = after(self.arrived, *due)

        def start(flags, mine, arrived):
            return [added_if(True, mine[...], arrived[...])]

        (total,) = small(start, self.flags, [self.mine, self.arrived], 1)
        self.rest_arrived = swap(after(self.mine, self.arrived), self.second)
        if rest_early:
            early = [self.rest_arrived, *early]
        before = None
        for index, bit in enumerate(self.rest, 2):
            last = bit == self.rest[-1]
            pieces = meanwhile(total) if last else list(early)
            arrived = after(swap(total, bit), *pieces)

            def first(flags, total, arrived):
                values = arrived[...], total[...]
                return [jnp.where(flags[counts + 2] == 1, values[0], 0.0), added_if(True, *values)]

            def middle(flags, total, arrived, before):
                value = added_if(flags[counts + index] == 1, before[...], arrived[...])
                return [value, added_if(True, total[...], arrived[...])]

            def final(flags, side, arrived, before):
                value = added_if(flags[counts + index] == 1, before[...], arrived[...])
                return [value, added_if(flags[counts + 1] == 1, value, side[...])]

            if before is None:
                before, total = small(first, self.flags, [total, arrived], 2)
            elif not last:
                before, total = small(middle, self.flags, [total, arrived, before], 2)
            else:
                self.before, self.own = small(final, self.flags, [self.arrived, arrived, before], 2)

    def collect(self):
        counts = self.counts

        def finish(flags, swapped, rest):
            return [added_if(flags[counts + 1] == 1, swapped[...], rest[...])]

        arrays = [swap(self.before, self.second), self.rest_arrived]
        (other,) = small(finish, self.flags, arrays, 1)
        quarters = [self.own, other, swap(self.own, self.first), swap(other, self.first)]
        self.operands = [("whole", self.other.reshape(-1, HEAD_DIM))]
        self.operands += [("held", quarter) for quarter in quarters]


def sides_kernel(flags_ref, in_ref, own_ref, gone_ref):
    columns = own_ref.shape[1]
    mine = flags_ref[flags_ref.shape[0] - 2]

    @pl.when(mine == 0)
    def _():
        own_ref[...] = in_ref[:, :columns]
        gone_ref[...] = in_ref[:, columns:]

    @pl.when(mine == 1)
    def _():
        own_ref[...] = in_ref[:, columns:]
        gone_ref[...] = in_ref[:, :columns]


def sides(array, flags):
    rows, columns = array.shape
    tile = rows // 2
    out = jax.ShapeDtypeStruct((rows, columns // 2), array.dtype)
    return pl.pallas_call(
        sides_kernel,
        grid_spec=pltpu.PrefetchScalarGridSpec(
            num_scalar_prefetch=1,
            grid=(rows // tile,),
            in_specs=[pl.BlockSpec((tile, columns), lambda i, flags: (i, 0))],
            out_specs=[pl.BlockSpec((tile, columns // 2), lambda i, flags: (i, 0))] * 2,
        ),
        out_shape=[out, out],
        compiler_params=pltpu.CompilerParams(vmem_limit_bytes=VMEM_MIB * 1024 * 1024),
        cost_estimate=pl.CostEstimate(flops=0, bytes_accessed=4 * array.size, transcendentals=0),
    )(flags, array)


def weight_kernel(sources_of, flags_ref, turned_ref, *refs):
    numbers = flags_ref.shape[0]
    mine, span = flags_ref[numbers - 2], flags_ref[numbers - 1]
    order = []
    for sequences, flips in sources_of:
        device = 0
        for bit, flip in enumerate(flips):
            device += 2**bit * (1 - flags_ref[bit] if flip else flags_ref[bit])
        pair = turned_ref.shape[0] == 16
        order += [8 * (lax.rem(mine + at, 2) if pair else at) + device for at in sequences]
    *held, kept_ref, sent_ref, total_ref, buffer_ref, arrival = refs
    sources, _, tokens = turned_ref.shape
    others, rows, columns = sent_ref.shape
    copies, at = [], 0
    for index, ref in enumerate(held):
        count = ref.shape[0]
        copies.append(pltpu.make_async_copy(ref, buffer_ref.at[at : at + count], arrival.at[index]))
        copies[-1].start()
        at += count
    per_step, tile = 4, 512 if columns % 512 == 0 else columns
    steps = sources // per_step
    for step in range(steps):
        for copy in copies[step * len(copies) // steps : (step + 1) * len(copies) // steps]:
            copy.wait()
        first = step * per_step
        lhs = jnp.concatenate([turned_ref[order[first + i]] for i in range(per_step)], axis=1)
        for start in range(0, columns, tile):
            cut = slice(start, start + tile)
            rhs = buffer_ref[first : first + per_step, :, cut].reshape(per_step * tokens, tile)
            product = dot(lhs, rhs, NN)
            total_ref[:, cut] = product if step == 0 else total_ref[:, cut] + product
    kept_ref[...] = total_ref[pl.ds(pl.multiple_of(span * rows, 16), rows), :]
    for turn in range(others):
        target = lax.rem(span + turn + 1, others + 1)
        sent_ref[turn] = total_ref[pl.ds(pl.multiple_of(target * rows, 16), rows), :].astype(BF16)


def weight_part(sources_of, flags, turned, inputs, halves):
    sources, rows, tokens = turned.shape
    columns = inputs[0].shape[-1]
    vmem = pl.BlockSpec(memory_space=pltpu.VMEM)
    return pl.pallas_call(
        functools.partial(weight_kernel, sources_of),
        in_specs=[pl.BlockSpec(memory_space=pltpu.SMEM), vmem]
        + [pl.BlockSpec(memory_space=pl.ANY)] * len(inputs),
        out_specs=[vmem, vmem],
        out_shape=[
            jax.ShapeDtypeStruct((rows // halves, columns), F32),
            jax.ShapeDtypeStruct((halves - 1, rows // halves, columns), BF16),
        ],
        scratch_shapes=[
            pltpu.VMEM((rows, columns), F32),
            pltpu.VMEM((sources, tokens, columns), BF16),
            pltpu.SemaphoreType.DMA((len(inputs),)),
        ],
        compiler_params=pltpu.CompilerParams(vmem_limit_bytes=VMEM_MIB * 1024 * 1024),
        cost_estimate=pl.CostEstimate(
            flops=2 * sources * tokens * rows * columns,
            bytes_accessed=sources * tokens * columns * 2 + rows * columns * 6,
            transcendentals=0,
        ),
    )(flags, turned, *inputs)


def shards(layer_input, query_rows, key_rows, value_rows, out_grad, bits):
    query, key, value, upstream = query_rows[0], key_rows[0], value_rows[0], out_grad[0]
    tokens, features = query.shape
    sequences = lax.axis_size("dp")
    places = 2 ** len(bits)
    core, side, layer, *high = bits
    spans = tuple(reversed(high))
    halves = places // 8
    cuts = 2
    rows = features // places // cuts

    place = [lax.axis_index(bit) for bit in bits]
    mine, span = lax.axis_index("dp"), lax.axis_index(spans)
    flags = jnp.stack(place + place + [1 - at for at in place] + [mine, span]).astype(jnp.int32)

    (block_state,) = by_heads(
        block_state_head, [("row", key), ("row", value)], [("held state", BF16)], 1, vmem=44
    )
    forward = Scan(block_state, bits, False, flags)

    if sequences == 2:
        own, gone = sides(after(layer_input[0], forward.mine), flags)
        own, far = own[None], swap(gone, "dp")[None]
    else:
        wide = lax.all_to_all(layer_input[0].reshape(tokens, sequences, -1), "dp", 1, 0)
        own, far = wide[: sequences // 2], wide[sequences // 2 :]

    far_side, far_both, output = [], [], []

    def along_side(token):
        far_side.append(swap(after(far, token), side))
        output.extend(
            by_heads(
                local_output_head,
                [("held", after(query, token)), ("held", key), ("held", value)],
                [("held row", F32)],
                2,
            )
        )
        return far_side + output

    forward.spread([], [far], along_side, True)
    forward.collect()
    far_layer = swap(after(far, forward.before), layer)
    grad_output, block_grad, state_in = by_heads(
        functools.partial(grad_output_head, forward.counts),
        [("held", query), ("held", output[0]), ("held", upstream), *forward.operands],
        [("held row", BF16), ("held state", BF16), ("state", BF16)],
        2,
        forward.flags,
    )
    own_layer = swap(after(own, block_grad), layer)
    backward = Scan(after(block_grad, far_layer), bits, True, flags)
    own_side = swap(after(own, backward.mine), side)
    (key_local,) = by_heads(
        key_local_head,
        [("held", query), ("held", value), ("held", after(grad_output, backward.mine))],
        [("held row", F32)],
        2,
    )

    def along_side_again(token):
        far_both.append(swap(after(far_layer, token), side))
        return far_both

    backward.spread([key_local], [own_side, own_layer], along_side_again, False)
    backward.collect()
    own_both = swap(after(own_side, backward.before), layer)
    key_grad, grad_in, *turned = by_heads(
        functools.partial(key_grad_head, backward.counts),
        [("held", key), ("held", value), ("held", key_local), *backward.operands],
        [("row", BF16), ("state", BF16)] + [((sequences, 8, halves, rows, tokens), BF16)] * cuts,
        1,
        after(backward.flags, own_both),
    )
    own_ids, far_ids = range(sequences // 2), range(sequences // 2, sequences)
    held, sources_of = [], []
    for array, ids, layered, sided in (
        (own, own_ids, 0, 0),
        (far, far_ids, 0, 0),
        (own_layer, own_ids, 1, 0),
        (far_layer, far_ids, 1, 0),
        (far_side[0], far_ids, 0, 1),
        (far_both[0], far_ids, 1, 1),
        (own_side, own_ids, 0, 1),
        (own_both, own_ids, 1, 1),
    ):
        held.append(array)
        sources_of.append((ids, (0, sided, layered)))
    held += [swap(array, core) for array in held]
    sources_of += [(ids, (1, sided, layered)) for ids, (_, sided, layered) in sources_of]
    turned[0] = after(turned[0], *held[8:])

    sums, done = [], turned[0]
    for cut in range(cuts):
        part = turned[cut].reshape(sequences * 8, halves * rows, tokens)
        part = lax.all_to_all(part, ("dp", layer, side, core), 0, 0, tiled=True)
        total, sent = weight_part(sources_of, flags, after(part, done), held, halves)
        for turn in range(1, halves):
            moved = lax.ppermute(sent[turn - 1], spans, [(i, (i + turn) % halves) for i in range(halves)])
            total += moved.astype(F32)
        done = sent
        sums.append(total)
    weight_grad = jnp.concatenate(sums) * (sequences * places * tokens) ** (-0.5)
    query_grad, value_grad = by_heads(
        other_grads_head,
        [
            ("held", query),
            ("held", key),
            ("held", value),
            ("held", after(grad_output, done)),
            ("state", state_in),
            ("state", grad_in),
        ],
        [("row", BF16), ("row", BF16)],
        6,
    )
    return (query_grad[None], key_grad[None], value_grad[None], weight_grad)


def solution(mesh):
    sequences, places = mesh.shape["dp"], mesh.shape["ctx"]
    bits = tuple(f"bit{i}" for i in range(places.bit_length() - 1))
    ctx = tuple(reversed(bits))
    devices = mesh.devices.reshape((sequences,) + (2,) * len(bits))
    rows = P("dp", ctx, None)
    return jax.shard_map(
        functools.partial(shards, bits=bits),
        mesh=jax.sharding.Mesh(devices, ("dp",) + ctx),
        in_specs=(rows,) * 5,
        out_specs=(rows, rows, rows, P(ctx, "dp")),
        check_vma=False,
    )
```

```python
import functools

import jax
import jax.numpy as jnp
from jax import lax
from jax.experimental import pallas as pl
from jax.experimental.pallas import tpu as pltpu
from jax.sharding import PartitionSpec as P

HEAD_DIM = 128
EPSILON = 1e-05
VMEM_MIB = 56
F32 = jnp.float32
BF16 = jnp.bfloat16

NN = (((1,), (0,)), ((), ()))
NT = (((1,), (1,)), ((), ()))
TN = (((0,), (0,)), ((), ()))


def dot(a, b, dims):
    return lax.dot_general(a, b, dims, preferred_element_type=F32)


def slope(values):
    wide = values.astype(F32)
    return jnp.where(wide > 0, 1.0, jnp.exp(jnp.minimum(wide, 0.0)))


def feature(values):
    wide = values.astype(F32)
    return jnp.where(wide > 0, wide + 1.0, jnp.exp(jnp.minimum(wide, 0.0))).astype(BF16)


def causal_scores(rows, columns):
    scores = dot(rows, columns, NT)
    t = lax.broadcasted_iota(jnp.int32, scores.shape, 0)
    s = lax.broadcasted_iota(jnp.int32, scores.shape, 1)
    return jnp.where(s <= t, scores, 0.0).astype(BF16)


def causal_scores_turned(rows, columns):
    scores = dot(columns, rows, NT)
    s = lax.broadcasted_iota(jnp.int32, scores.shape, 0)
    t = lax.broadcasted_iota(jnp.int32, scores.shape, 1)
    return jnp.where(s <= t, scores, 0.0).astype(BF16)


def block_state_head(at, k_ref, v_ref, state_ref):
    state_ref[at, :] = dot(feature(k_ref[:, at]), v_ref[:, at], TN).astype(BF16)


def local_output_head(at, q_ref, k_ref, v_ref, local_ref):
    scores = causal_scores(feature(q_ref[:, at]), feature(k_ref[:, at]))
    local_ref[:, at] = dot(scores, v_ref[:, at], NN)


def assemble(at, counts, flags_ref, other_ref, quarter_refs, state_ref):
    size = quarter_refs[0].shape[0]
    quarter, start = divmod(at.start, size)
    near = flags_ref[0] == quarter // 2
    same = flags_ref[1] == quarter % 2
    own, other, swapped_own, swapped_other = [ref[start : start + HEAD_DIM, :] for ref in quarter_refs]
    total = jnp.where(same, jnp.where(near, own, swapped_own), jnp.where(near, other, swapped_other))
    total = added_if(flags_ref[counts] == 1, total, other_ref[at, :])
    state_ref[at, :] = total
    return total


def grad_output_head(counts, at, flags_ref, q_ref, local_ref, upstream_ref, other_ref, *refs):
    *quarter_refs, grad_ref, block_ref, state_ref = refs
    state = assemble(at, counts, flags_ref, other_ref, quarter_refs, state_ref)
    query = feature(q_ref[:, at])
    output = local_ref[:, at] + dot(query, state, NN)
    inverse_rms = lax.rsqrt(jnp.mean(output * output, axis=-1, keepdims=True) + EPSILON)
    normed = output * inverse_rms
    upstream = upstream_ref[:, at].astype(F32)
    projection = jnp.mean(upstream * normed, axis=-1, keepdims=True)
    grad = (inverse_rms * (upstream - normed * projection)).astype(BF16)
    grad_ref[:, at] = grad
    block_ref[at, :] = dot(query, grad, TN).astype(BF16)


def key_local_head(at, q_ref, v_ref, grad_ref, key_out):
    grad_scores = causal_scores_turned(grad_ref[:, at], v_ref[:, at])
    key_out[:, at] = dot(grad_scores, feature(q_ref[:, at]), NN)


def key_grad_head(counts, at, flags_ref, k_ref, v_ref, local_ref, other_ref, *refs):
    *quarter_refs, key_out, state_ref = refs[:6]
    turned_out = refs[6:]
    cuts = len(turned_out)
    copies, devices, halves, rows, tokens = turned_out[0].shape
    state = assemble(at, counts, flags_ref, other_ref, quarter_refs, state_ref)
    key = local_ref[:, at] + dot(v_ref[:, at], state, NT)
    key = (key * slope(k_ref[:, at])).astype(BF16)
    key_out[:, at] = key
    turned = key.T
    start = at.start
    while start < at.stop:
        block, row = divmod(start, rows)
        size = min(rows - row, at.stop - start)
        owner, cut = divmod(block, cuts)
        half, device = divmod(owner, devices)
        for copy in range(copies):
            turned_out[cut][copy, device, half, row : row + size] = turned[start - at.start : start - at.start + size]
        start += size


def other_grads_head(at, q_ref, k_ref, v_ref, grad_ref, state_ref, later_ref, query_out, value_out):
    grad = grad_ref[:, at]
    key = feature(k_ref[:, at])
    grad_scores = causal_scores(grad, v_ref[:, at])
    query = dot(grad_scores, key, NN) + dot(grad, state_ref[at, :], NT)
    query_out[:, at] = (query * slope(q_ref[:, at])).astype(BF16)
    scores = causal_scores_turned(feature(q_ref[:, at]), key)
    value = dot(scores, grad, NN) + dot(key, later_ref[at, :], NN)
    value_out[:, at] = value.astype(BF16)


def by_heads(head, operands, outs, matmuls, bits=None, vmem=12):
    tokens, features = operands[0][1].shape
    groups = 2 if features % (2 * HEAD_DIM) == 0 else 1
    group = features // groups
    shapes = {"row": (tokens, features), "state": (features, HEAD_DIM)}
    shapes_held = {"held row": shapes["row"], "held state": shapes["state"]}
    kinds = [kind for kind, _ in operands] + [kind for kind, _ in outs]
    results = [
        jax.ShapeDtypeStruct(shapes.get(kind) or shapes_held.get(kind, kind), dtype) for kind, dtype in outs
    ]
    held = [kind == "held" or kind in shapes_held for kind in kinds]
    arrays = [array for _, array in operands] + results
    count = len(operands)

    def part(kind, ref, index):
        cut = pl.ds(index * group, group)
        return ref.at[:, cut] if kind == "row" else ref.at[cut, :]

    def body(*refs):
        numbers = [] if bits is None else [numbers_of(bits)]
        there, moved = refs[: len(kinds)], refs[-1]
        scratch = iter(refs[len(kinds) : -1])
        here = [ref if stays else next(scratch) for stays, ref in zip(held, there)]

        def copy(index, step):
            source, target = (there, here) if index < count else (here, there)
            source, target = source[index], target[index]
            if kinds[index] in shapes:
                source, target = part(kinds[index], source, step), part(kinds[index], target, step)
            return pltpu.make_async_copy(source, target, moved.at[index, step])

        def at_once(index, step):
            return step == (0 if index < count else groups - 1)

        def due(step, indices):
            moving = [index for index in indices if not held[index]]
            return [index for index in moving if kinds[index] in shapes or at_once(index, step)]

        ins, outputs = range(count), range(count, len(kinds))
        for step in range(groups):
            for index in due(step, ins):
                copy(index, step).start()
        for step in range(groups):
            for index in due(step, ins):
                copy(index, step).wait()
            for start in range(step * group, (step + 1) * group, HEAD_DIM):
                head(slice(start, start + HEAD_DIM), *numbers, *here)
            for index in due(step, outputs):
                copy(index, step).start()
        for step in range(groups):
            for index in due(step, outputs):
                copy(index, step).wait()

    anywhere = pl.BlockSpec(memory_space=pl.ANY)
    places = [pl.BlockSpec(memory_space=pltpu.VMEM) if stays else anywhere for stays in held]
    return pl.pallas_call(
        body,
        in_specs=places[:count],
        out_specs=places[count:],
        out_shape=results,
        scratch_shapes=[
            pltpu.VMEM(array.shape, array.dtype) for stays, array in zip(held, arrays) if not stays
        ]
        + [pltpu.SemaphoreType.DMA((len(kinds), groups))],
        compiler_params=pltpu.CompilerParams(vmem_limit_bytes=vmem * 1024 * 1024),
        cost_estimate=pl.CostEstimate(
            flops=2 * matmuls * tokens * features * HEAD_DIM,
            bytes_accessed=tokens * features * 2 * len(kinds),
            transcendentals=0,
        ),
    )(*[array for _, array in operands])


def swap(array, axis):
    return lax.ppermute(array, axis, [(0, 1), (1, 0)])


def numbers_of(bits):
    place = [lax.axis_index(bit) for bit in bits]
    span = sum(2**index * at for index, at in enumerate(place[3:]))
    return place + place + [1 - at for at in place] + [lax.axis_index("dp"), span]


def added_if(flag, a, b):
    return (a.astype(F32) + jnp.where(flag, b.astype(F32), 0.0)).astype(BF16)


def small(body, bits, arrays, outs):
    vmem = pl.BlockSpec(memory_space=pltpu.VMEM)
    result = jax.ShapeDtypeStruct(arrays[-1].shape[-2:], BF16)

    def kernel(*refs):
        values = body(numbers_of(bits), *refs[: len(arrays)])
        for ref, value in zip(refs[len(arrays) :], values):
            ref[...] = value

    return pl.pallas_call(
        kernel,
        in_specs=[vmem] * len(arrays),
        out_specs=[vmem] * outs,
        out_shape=[result] * outs,
        compiler_params=pltpu.CompilerParams(vmem_limit_bytes=4 * 1024 * 1024),
        cost_estimate=pl.CostEstimate(flops=0, bytes_accessed=1024, transcendentals=0),
    )(*arrays)


def after(array, *others):
    if not others:
        return array
    return lax.optimization_barrier((array,) + others)[0]


class Scan:
    def __init__(self, state, bits, backward):
        first, second, *self.rest = bits
        self.first, self.second = first, second
        self.bits, self.counts = bits, (2 if backward else 1) * len(bits)
        state = state.reshape(2, 2, -1, HEAD_DIM)
        self.other = swap(state, first)

        def quarters(flags, state, other):
            core, side = flags[0], flags[1]
            return [added_if(True, state[core, at], other[core, at]) for at in (1 - side, side)]

        self.theirs, self.mine = small(quarters, self.bits, [state, self.other], 2)
        self.arrived = swap(self.theirs, second)

    def spread(self, due, early, meanwhile, rest_early):
        counts = self.counts
        self.arrived = after(self.arrived, *due)

        def start(flags, mine, arrived):
            return [added_if(True, mine[...], arrived[...])]

        (total,) = small(start, self.bits, [self.mine, self.arrived], 1)
        self.rest_arrived = swap(after(self.mine, self.arrived), self.second)
        if rest_early:
            early = [self.rest_arrived, *early]
        before = None
        for index, bit in enumerate(self.rest, 2):
            last = bit == self.rest[-1]
            pieces = meanwhile(total) if last else list(early)
            arrived = after(swap(total, bit), *pieces)

            def first(flags, total, arrived):
                values = arrived[...], total[...]
                return [jnp.where(flags[counts + 2] == 1, values[0], 0.0), added_if(True, *values)]

            def middle(flags, total, arrived, before):
                value = added_if(flags[counts + index] == 1, before[...], arrived[...])
                return [value, added_if(True, total[...], arrived[...])]

            def final(flags, side, arrived, before):
                value = added_if(flags[counts + index] == 1, before[...], arrived[...])
                return [value, added_if(flags[counts + 1] == 1, value, side[...])]

            if before is None:
                before, total = small(first, self.bits, [total, arrived], 2)
            elif not last:
                before, total = small(middle, self.bits, [total, arrived, before], 2)
            else:
                self.before, self.own = small(final, self.bits, [self.arrived, arrived, before], 2)

    def collect(self):
        counts = self.counts

        def finish(flags, swapped, rest):
            return [added_if(flags[counts + 1] == 1, swapped[...], rest[...])]

        arrays = [swap(self.before, self.second), self.rest_arrived]
        (other,) = small(finish, self.bits, arrays, 1)
        quarters = [self.own, other, swap(self.own, self.first), swap(other, self.first)]
        self.operands = [("whole", self.other.reshape(-1, HEAD_DIM))]
        self.operands += [("held", quarter) for quarter in quarters]


def sides_kernel(in_ref, own_ref, gone_ref):
    columns = own_ref.shape[1]
    mine = lax.axis_index("dp")

    @pl.when(mine == 0)
    def _():
        own_ref[...] = in_ref[:, :columns]
        gone_ref[...] = in_ref[:, columns:]

    @pl.when(mine == 1)
    def _():
        own_ref[...] = in_ref[:, columns:]
        gone_ref[...] = in_ref[:, :columns]


def sides(array):
    rows, columns = array.shape
    tile = rows // 2
    out = jax.ShapeDtypeStruct((rows, columns // 2), array.dtype)
    return pl.pallas_call(
        sides_kernel,
        grid=(rows // tile,),
        in_specs=[pl.BlockSpec((tile, columns), lambda i: (i, 0))],
        out_specs=[pl.BlockSpec((tile, columns // 2), lambda i: (i, 0))] * 2,
        out_shape=[out, out],
        compiler_params=pltpu.CompilerParams(vmem_limit_bytes=VMEM_MIB * 1024 * 1024),
        cost_estimate=pl.CostEstimate(flops=0, bytes_accessed=4 * array.size, transcendentals=0),
    )(array)


def weight_kernel(sources_of, bits, turned_in, *refs):
    *numbers, mine, span = numbers_of(bits)
    order = []
    for sequences, flips in sources_of:
        device = 0
        for bit, flip in enumerate(flips):
            device += 2**bit * (1 - numbers[bit] if flip else numbers[bit])
        pair = turned_in.shape[0] == 16
        order += [8 * (lax.rem(mine + at, 2) if pair else at) + device for at in sequences]
    *held, kept_out, sent_out, total_ref, turned_ref, buffer_ref, kept_ref, sent_ref, arrival, departure = refs
    sources, _, tokens = turned_ref.shape
    others, rows, columns = sent_ref.shape
    turning = pltpu.make_async_copy(turned_in, turned_ref, arrival.at[len(held)])
    turning.start()
    copies, at = [], 0
    for index, ref in enumerate(held):
        count = ref.shape[0]
        copies.append(pltpu.make_async_copy(ref, buffer_ref.at[at : at + count], arrival.at[index]))
        copies[-1].start()
        at += count
    per_step, tile = 4, 512 if columns % 512 == 0 else columns
    steps = sources // per_step
    leaving = []
    turning.wait()
    for step in range(steps):
        for copy in copies[step * len(copies) // steps : (step + 1) * len(copies) // steps]:
            copy.wait()
        first = step * per_step
        lhs = jnp.concatenate([turned_ref[order[first + i]] for i in range(per_step)], axis=1)
        for index, start in enumerate(range(0, columns, tile)):
            cut = slice(start, start + tile)
            rhs = buffer_ref[first : first + per_step, :, cut].reshape(per_step * tokens, tile)
            product = dot(lhs, rhs, NN)
            total_ref[:, cut] = product if step == 0 else total_ref[:, cut] + product
            if step < steps - 1:
                continue
            kept_ref[:, cut] = total_ref[pl.ds(pl.multiple_of(span * rows, 16), rows), cut]
            for turn in range(others):
                target = lax.rem(span + turn + 1, others + 1)
                sent_ref[turn, :, cut] = total_ref[pl.ds(pl.multiple_of(target * rows, 16), rows), cut].astype(BF16)
            there = pl.ds(start, tile)
            leaving += [
                pltpu.make_async_copy(kept_ref.at[:, there], kept_out.at[:, there], departure.at[0, index]),
                pltpu.make_async_copy(sent_ref.at[:, :, there], sent_out.at[:, :, there], departure.at[1, index]),
            ]
            leaving[-2].start()
            leaving[-1].start()
    for copy in leaving:
        copy.wait()


def weight_part(sources_of, bits, turned, inputs, halves):
    sources, rows, tokens = turned.shape
    columns = inputs[0].shape[-1]
    return pl.pallas_call(
        functools.partial(weight_kernel, sources_of, bits),
        in_specs=[pl.BlockSpec(memory_space=pl.ANY)] * (1 + len(inputs)),
        out_specs=[pl.BlockSpec(memory_space=pl.ANY)] * 2,
        out_shape=[
            jax.ShapeDtypeStruct((rows // halves, columns), F32),
            jax.ShapeDtypeStruct((halves - 1, rows // halves, columns), BF16),
        ],
        scratch_shapes=[
            pltpu.VMEM((rows, columns), F32),
            pltpu.VMEM(turned.shape, BF16),
            pltpu.VMEM((sources, tokens, columns), BF16),
            pltpu.VMEM((rows // halves, columns), F32),
            pltpu.VMEM((halves - 1, rows // halves, columns), BF16),
            pltpu.SemaphoreType.DMA((len(inputs) + 1,)),
            pltpu.SemaphoreType.DMA((2, max(columns // 512, 1))),
        ],
        compiler_params=pltpu.CompilerParams(vmem_limit_bytes=VMEM_MIB * 1024 * 1024),
        cost_estimate=pl.CostEstimate(
            flops=2 * sources * tokens * rows * columns,
            bytes_accessed=sources * tokens * columns * 2 + rows * columns * 6,
            transcendentals=0,
        ),
    )(turned, *inputs)


def shards(layer_input, query_rows, key_rows, value_rows, out_grad, bits):
    query, key, value, upstream = query_rows[0], key_rows[0], value_rows[0], out_grad[0]
    tokens, features = query.shape
    sequences = lax.axis_size("dp")
    places = 2 ** len(bits)
    core, side, layer, *high = bits
    spans = tuple(reversed(high))
    halves = places // 8
    cuts = 2
    rows = features // places // cuts

    (block_state,) = by_heads(
        block_state_head, [("row", key), ("row", value)], [("held state", BF16)], 1, vmem=44
    )
    forward = Scan(block_state, bits, False)

    if sequences == 2:
        own, gone = sides(after(layer_input[0], forward.mine))
        own, far = own[None], swap(gone, "dp")[None]
    else:
        wide = lax.all_to_all(layer_input[0].reshape(tokens, sequences, -1), "dp", 1, 0)
        own, far = wide[: sequences // 2], wide[sequences // 2 :]

    far_side, far_both, output = [], [], []

    def along_side(token):
        far_side.append(swap(after(far, token), side))
        output.extend(
            by_heads(
                local_output_head,
                [("held", after(query, token)), ("held", key), ("held", value)],
                [("held row", F32)],
                2,
            )
        )
        return far_side + output

    forward.spread([], [far], along_side, True)
    forward.collect()
    far_layer = swap(after(far, forward.before), layer)
    grad_output, block_grad, state_in = by_heads(
        functools.partial(grad_output_head, forward.counts),
        [("held", query), ("held", output[0]), ("held", upstream), *forward.operands],
        [("held row", BF16), ("held state", BF16), ("state", BF16)],
        2,
        bits,
    )
    own_layer = swap(after(own, block_grad), layer)
    backward = Scan(after(block_grad, far_layer), bits, True)
    own_side = swap(after(own, backward.mine), side)
    (key_local,) = by_heads(
        key_local_head,
        [("held", query), ("held", value), ("held", after(grad_output, backward.mine))],
        [("held row", F32)],
        2,
    )

    def along_side_again(token):
        far_both.append(swap(after(far_layer, token), side))
        return far_both

    backward.spread([key_local], [own_side, own_layer], along_side_again, False)
    backward.collect()
    own_both = swap(after(own_side, backward.before), layer)
    key_grad, grad_in, *turned = by_heads(
        functools.partial(key_grad_head, backward.counts),
        [("held", after(key, own_both)), ("held", value), ("held", key_local), *backward.operands],
        [("row", BF16), ("state", BF16)] + [((sequences, 8, halves, rows, tokens), BF16)] * cuts,
        1,
        bits,
    )
    own_ids, far_ids = range(sequences // 2), range(sequences // 2, sequences)
    held, sources_of = [], []
    for array, ids, layered, sided in (
        (own, own_ids, 0, 0),
        (far, far_ids, 0, 0),
        (own_layer, own_ids, 1, 0),
        (far_layer, far_ids, 1, 0),
        (far_side[0], far_ids, 0, 1),
        (far_both[0], far_ids, 1, 1),
        (own_side, own_ids, 0, 1),
        (own_both, own_ids, 1, 1),
    ):
        held.append(array)
        sources_of.append((ids, (0, sided, layered)))
    held += [swap(array, core) for array in held]
    sources_of += [(ids, (1, sided, layered)) for ids, (_, sided, layered) in sources_of]
    turned[0] = after(turned[0], *held[8:])

    sums, done = [], turned[0]
    for cut in range(cuts):
        part = turned[cut].reshape(sequences * 8, halves * rows, tokens)
        part = lax.all_to_all(part, ("dp", layer, side, core), 0, 0, tiled=True)
        total, sent = weight_part(sources_of, bits, after(part, done), held, halves)
        for turn in range(1, halves):
            moved = lax.ppermute(sent[turn - 1], spans, [(i, (i + turn) % halves) for i in range(halves)])
            total += moved.astype(F32)
        done = sent
        sums.append(total)
    weight_grad = jnp.concatenate(sums) * (sequences * places * tokens) ** (-0.5)
    query_grad, value_grad = by_heads(
        other_grads_head,
        [
            ("held", query),
            ("held", key),
            ("held", value),
            ("held", after(grad_output, done)),
            ("state", state_in),
            ("state", grad_in),
        ],
        [("row", BF16), ("row", BF16)],
        6,
    )
    return (query_grad[None], key_grad[None], value_grad[None], weight_grad)


def solution(mesh):
    sequences, places = mesh.shape["dp"], mesh.shape["ctx"]
    bits = tuple(f"bit{i}" for i in range(places.bit_length() - 1))
    ctx = tuple(reversed(bits))
    devices = mesh.devices.reshape((sequences,) + (2,) * len(bits))
    rows = P("dp", ctx, None)
    return jax.shard_map(
        functools.partial(shards, bits=bits),
        mesh=jax.sharding.Mesh(devices, ("dp",) + ctx),
        in_specs=(rows,) * 5,
        out_specs=(rows, rows, rows, P(ctx, "dp")),
        check_vma=False,
    )
```

```python
import functools

import jax
import jax.numpy as jnp
from jax import lax
from jax.experimental import pallas as pl
from jax.experimental.pallas import tpu as pltpu
from jax.sharding import PartitionSpec as P

HEAD_DIM = 128
EPSILON = 1e-05
VMEM_MIB = 56
F32 = jnp.float32
BF16 = jnp.bfloat16

NN = (((1,), (0,)), ((), ()))
NT = (((1,), (1,)), ((), ()))
TN = (((0,), (0,)), ((), ()))


def dot(a, b, dims):
    return lax.dot_general(a, b, dims, preferred_element_type=F32)


def slope(values):
    wide = values.astype(F32)
    return jnp.where(wide > 0, 1.0, jnp.exp(jnp.minimum(wide, 0.0)))


def feature(values):
    wide = values.astype(F32)
    return jnp.where(wide > 0, wide + 1.0, jnp.exp(jnp.minimum(wide, 0.0))).astype(BF16)


def causal_scores(rows, columns):
    scores = dot(rows, columns, NT)
    t = lax.broadcasted_iota(jnp.int32, scores.shape, 0)
    s = lax.broadcasted_iota(jnp.int32, scores.shape, 1)
    return jnp.where(s <= t, scores, 0.0).astype(BF16)


def causal_scores_turned(rows, columns):
    scores = dot(columns, rows, NT)
    s = lax.broadcasted_iota(jnp.int32, scores.shape, 0)
    t = lax.broadcasted_iota(jnp.int32, scores.shape, 1)
    return jnp.where(s <= t, scores, 0.0).astype(BF16)


def block_state_head(at, k_ref, v_ref, state_ref):
    state_ref[at, :] = dot(feature(k_ref[:, at]), v_ref[:, at], TN).astype(BF16)


def local_output_head(at, q_ref, k_ref, v_ref, local_ref):
    scores = causal_scores(feature(q_ref[:, at]), feature(k_ref[:, at]))
    local_ref[:, at] = dot(scores, v_ref[:, at], NN)


def assemble(at, counts, flags_ref, other_ref, quarter_refs):
    size = quarter_refs[0].shape[0]
    quarter, start = divmod(at.start, size)
    near = flags_ref[0] == quarter // 2
    same = flags_ref[1] == quarter % 2
    own, other, swapped_own, swapped_other = [ref[start : start + HEAD_DIM, :] for ref in quarter_refs]
    total = jnp.where(same, jnp.where(near, own, swapped_own), jnp.where(near, other, swapped_other))
    return added_if(flags_ref[counts] == 1, total, other_ref[at, :])


def grad_output_head(counts, at, flags_ref, q_ref, local_ref, upstream_ref, other_ref, *refs):
    *quarter_refs, grad_ref, block_ref, state_ref = refs
    state = assemble(at, counts, flags_ref, other_ref, quarter_refs)
    state_ref[at, :] = state
    query = feature(q_ref[:, at])
    output = local_ref[:, at] + dot(query, state, NN)
    inverse_rms = lax.rsqrt(jnp.mean(output * output, axis=-1, keepdims=True) + EPSILON)
    normed = output * inverse_rms
    upstream = upstream_ref[:, at].astype(F32)
    projection = jnp.mean(upstream * normed, axis=-1, keepdims=True)
    grad = (inverse_rms * (upstream - normed * projection)).astype(BF16)
    grad_ref[:, at] = grad
    block_ref[at, :] = dot(query, grad, TN).astype(BF16)


def key_local_head(at, q_ref, v_ref, grad_ref, key_out):
    grad_scores = causal_scores_turned(grad_ref[:, at], v_ref[:, at])
    key_out[:, at] = dot(grad_scores, feature(q_ref[:, at]), NN)


def key_grad_head(counts, at, flags_ref, k_ref, v_ref, local_ref, other_ref, *refs):
    *quarter_refs, key_out = refs[:5]
    turned_out = refs[5:]
    cuts = len(turned_out)
    copies, devices, halves, rows, tokens = turned_out[0].shape
    state = assemble(at, counts, flags_ref, other_ref, quarter_refs)
    key = local_ref[:, at] + dot(v_ref[:, at], state, NT)
    key = (key * slope(k_ref[:, at])).astype(BF16)
    key_out[:, at] = key
    turned = key.T
    start = at.start
    while start < at.stop:
        block, row = divmod(start, rows)
        size = min(rows - row, at.stop - start)
        owner, cut = divmod(block, cuts)
        half, device = divmod(owner, devices)
        for copy in range(copies):
            turned_out[cut][copy, device, half, row : row + size] = turned[start - at.start : start - at.start + size]
        start += size


def other_grads_head(counts, at, flags_ref, q_ref, k_ref, v_ref, grad_ref, state_ref, other_ref, *refs):
    *quarter_refs, query_out, value_out = refs
    later = assemble(at, counts, flags_ref, other_ref, quarter_refs)
    grad = grad_ref[:, at]
    key = feature(k_ref[:, at])
    grad_scores = causal_scores(grad, v_ref[:, at])
    query = dot(grad_scores, key, NN) + dot(grad, state_ref[at, :], NT)
    query_out[:, at] = (query * slope(q_ref[:, at])).astype(BF16)
    scores = causal_scores_turned(feature(q_ref[:, at]), key)
    value = dot(scores, grad, NN) + dot(key, later, NN)
    value_out[:, at] = value.astype(BF16)


def by_heads(head, operands, outs, matmuls, bits=None, vmem=12):
    tokens, features = operands[0][1].shape
    groups = 2 if features % (2 * HEAD_DIM) == 0 else 1
    group = features // groups
    shapes = {"row": (tokens, features), "state": (features, HEAD_DIM)}
    shapes_held = {"held row": shapes["row"], "held state": shapes["state"]}
    kinds = [kind for kind, _ in operands] + [kind for kind, _ in outs]
    results = [
        jax.ShapeDtypeStruct(shapes.get(kind) or shapes_held.get(kind, kind), dtype) for kind, dtype in outs
    ]
    held = [kind == "held" or kind in shapes_held for kind in kinds]
    arrays = [array for _, array in operands] + results
    count = len(operands)

    def part(kind, ref, index):
        cut = pl.ds(index * group, group)
        return ref.at[:, cut] if kind == "row" else ref.at[cut, :]

    def body(*refs):
        numbers = [] if bits is None else [numbers_of(bits)]
        there, moved = refs[: len(kinds)], refs[-1]
        scratch = iter(refs[len(kinds) : -1])
        here = [ref if stays else next(scratch) for stays, ref in zip(held, there)]

        def copy(index, step):
            source, target = (there, here) if index < count else (here, there)
            source, target = source[index], target[index]
            if kinds[index] in shapes:
                source, target = part(kinds[index], source, step), part(kinds[index], target, step)
            return pltpu.make_async_copy(source, target, moved.at[index, step])

        def at_once(index, step):
            return step == (0 if index < count else groups - 1)

        def due(step, indices):
            moving = [index for index in indices if not held[index]]
            return [index for index in moving if kinds[index] in shapes or at_once(index, step)]

        ins, outputs = range(count), range(count, len(kinds))
        for step in range(groups):
            for index in due(step, ins):
                copy(index, step).start()
        for step in range(groups):
            for index in due(step, ins):
                copy(index, step).wait()
            for start in range(step * group, (step + 1) * group, HEAD_DIM):
                head(slice(start, start + HEAD_DIM), *numbers, *here)
            for index in due(step, outputs):
                copy(index, step).start()
        for step in range(groups):
            for index in due(step, outputs):
                copy(index, step).wait()

    anywhere = pl.BlockSpec(memory_space=pl.ANY)
    places = [pl.BlockSpec(memory_space=pltpu.VMEM) if stays else anywhere for stays in held]
    return pl.pallas_call(
        body,
        in_specs=places[:count],
        out_specs=places[count:],
        out_shape=results,
        scratch_shapes=[
            pltpu.VMEM(array.shape, array.dtype) for stays, array in zip(held, arrays) if not stays
        ]
        + [pltpu.SemaphoreType.DMA((len(kinds), groups))],
        compiler_params=pltpu.CompilerParams(vmem_limit_bytes=vmem * 1024 * 1024),
        cost_estimate=pl.CostEstimate(
            flops=2 * matmuls * tokens * features * HEAD_DIM,
            bytes_accessed=tokens * features * 2 * len(kinds),
            transcendentals=0,
        ),
    )(*[array for _, array in operands])


def swap(array, axis):
    return lax.ppermute(array, axis, [(0, 1), (1, 0)])


def numbers_of(bits):
    place = [lax.axis_index(bit) for bit in bits]
    span = sum(2**index * at for index, at in enumerate(place[3:]))
    return place + place + [1 - at for at in place] + [lax.axis_index("dp"), span]


def added_if(flag, a, b):
    return (a.astype(F32) + jnp.where(flag, b.astype(F32), 0.0)).astype(BF16)


def small(body, bits, arrays, outs):
    vmem = pl.BlockSpec(memory_space=pltpu.VMEM)
    result = jax.ShapeDtypeStruct(arrays[-1].shape[-2:], BF16)

    def kernel(*refs):
        values = body(numbers_of(bits), *refs[: len(arrays)])
        for ref, value in zip(refs[len(arrays) :], values):
            ref[...] = value

    return pl.pallas_call(
        kernel,
        in_specs=[vmem] * len(arrays),
        out_specs=[vmem] * outs,
        out_shape=[result] * outs,
        compiler_params=pltpu.CompilerParams(vmem_limit_bytes=4 * 1024 * 1024),
        cost_estimate=pl.CostEstimate(flops=0, bytes_accessed=1024, transcendentals=0),
    )(*arrays)


def after(array, *others):
    if not others:
        return array
    return lax.optimization_barrier((array,) + others)[0]


class Scan:
    def __init__(self, state, bits, backward):
        first, second, *self.rest = bits
        self.first, self.second = first, second
        self.bits, self.counts = bits, (2 if backward else 1) * len(bits)
        state = state.reshape(2, 2, -1, HEAD_DIM)
        self.other = swap(state, first)

        def quarters(flags, state, other):
            core, side = flags[0], flags[1]
            return [added_if(True, state[core, at], other[core, at]) for at in (1 - side, side)]

        self.theirs, self.mine = small(quarters, self.bits, [state, self.other], 2)
        self.arrived = swap(self.theirs, second)

    def spread(self, due, early, meanwhile, rest_early):
        counts = self.counts
        self.arrived = after(self.arrived, *due)

        def start(flags, mine, arrived):
            return [added_if(True, mine[...], arrived[...])]

        (total,) = small(start, self.bits, [self.mine, self.arrived], 1)
        self.rest_arrived = swap(after(self.mine, self.arrived), self.second)
        if rest_early:
            early = [self.rest_arrived, *early]
        before = None
        for index, bit in enumerate(self.rest, 2):
            last = bit == self.rest[-1]
            pieces = meanwhile(total) if last else list(early)
            arrived = after(swap(total, bit), *pieces)

            def first(flags, total, arrived):
                values = arrived[...], total[...]
                return [jnp.where(flags[counts + 2] == 1, values[0], 0.0), added_if(True, *values)]

            def middle(flags, total, arrived, before):
                value = added_if(flags[counts + index] == 1, before[...], arrived[...])
                return [value, added_if(True, total[...], arrived[...])]

            def final(flags, side, arrived, before):
                value = added_if(flags[counts + index] == 1, before[...], arrived[...])
                return [value, added_if(flags[counts + 1] == 1, value, side[...])]

            if before is None:
                before, total = small(first, self.bits, [total, arrived], 2)
            elif not last:
                before, total = small(middle, self.bits, [total, arrived, before], 2)
            else:
                self.before, self.own = small(final, self.bits, [self.arrived, arrived, before], 2)

    def collect(self):
        counts = self.counts

        def finish(flags, swapped, rest):
            return [added_if(flags[counts + 1] == 1, swapped[...], rest[...])]

        arrays = [swap(self.before, self.second), self.rest_arrived]
        (other,) = small(finish, self.bits, arrays, 1)
        quarters = [self.own, other, swap(self.own, self.first), swap(other, self.first)]
        self.operands = [("whole", self.other.reshape(-1, HEAD_DIM))]
        self.operands += [("held", quarter) for quarter in quarters]


def sides_kernel(in_ref, own_ref, gone_ref):
    columns = own_ref.shape[1]
    mine = lax.axis_index("dp")

    @pl.when(mine == 0)
    def _():
        own_ref[...] = in_ref[:, :columns]
        gone_ref[...] = in_ref[:, columns:]

    @pl.when(mine == 1)
    def _():
        own_ref[...] = in_ref[:, columns:]
        gone_ref[...] = in_ref[:, :columns]


def sides(array):
    rows, columns = array.shape
    tile = rows // 2
    out = jax.ShapeDtypeStruct((rows, columns // 2), array.dtype)
    return pl.pallas_call(
        sides_kernel,
        grid=(rows // tile,),
        in_specs=[pl.BlockSpec((tile, columns), lambda i: (i, 0))],
        out_specs=[pl.BlockSpec((tile, columns // 2), lambda i: (i, 0))] * 2,
        out_shape=[out, out],
        compiler_params=pltpu.CompilerParams(vmem_limit_bytes=VMEM_MIB * 1024 * 1024),
        cost_estimate=pl.CostEstimate(flops=0, bytes_accessed=4 * array.size, transcendentals=0),
    )(array)


def weight_kernel(sources_of, bits, turned_in, *refs):
    *numbers, mine, span = numbers_of(bits)
    order = []
    for sequences, flips in sources_of:
        device = 0
        for bit, flip in enumerate(flips):
            device += 2**bit * (1 - numbers[bit] if flip else numbers[bit])
        pair = turned_in.shape[0] == 16
        order += [8 * (lax.rem(mine + at, 2) if pair else at) + device for at in sequences]
    *held, kept_out, sent_out, total_ref, turned_ref, buffer_ref, kept_ref, sent_ref, arrival, departure = refs
    sources, _, tokens = turned_ref.shape
    others, rows, columns = sent_ref.shape
    turning = pltpu.make_async_copy(turned_in, turned_ref, arrival.at[len(held)])
    turning.start()
    copies, at = [], 0
    for index, ref in enumerate(held):
        count = ref.shape[0]
        copies.append(pltpu.make_async_copy(ref, buffer_ref.at[at : at + count], arrival.at[index]))
        copies[-1].start()
        at += count
    per_step, tile = 4, 512 if columns % 512 == 0 else columns
    steps = sources // per_step
    leaving = []
    turning.wait()
    for step in range(steps):
        for copy in copies[step * len(copies) // steps : (step + 1) * len(copies) // steps]:
            copy.wait()
        first = step * per_step
        lhs = jnp.concatenate([turned_ref[order[first + i]] for i in range(per_step)], axis=1)
        for index, start in enumerate(range(0, columns, tile)):
            cut = slice(start, start + tile)
            rhs = buffer_ref[first : first + per_step, :, cut].reshape(per_step * tokens, tile)
            product = dot(lhs, rhs, NN)
            total_ref[:, cut] = product if step == 0 else total_ref[:, cut] + product
            if step < steps - 1:
                continue
            kept_ref[:, cut] = total_ref[pl.ds(pl.multiple_of(span * rows, 16), rows), cut]
            for turn in range(others):
                target = lax.rem(span + turn + 1, others + 1)
                sent_ref[turn, :, cut] = total_ref[pl.ds(pl.multiple_of(target * rows, 16), rows), cut].astype(BF16)
            there = pl.ds(start, tile)
            leaving += [
                pltpu.make_async_copy(kept_ref.at[:, there], kept_out.at[:, there], departure.at[0, index]),
                pltpu.make_async_copy(sent_ref.at[:, :, there], sent_out.at[:, :, there], departure.at[1, index]),
            ]
            leaving[-2].start()
            leaving[-1].start()
    for copy in leaving:
        copy.wait()


def weight_part(sources_of, bits, turned, inputs, halves):
    sources, rows, tokens = turned.shape
    columns = inputs[0].shape[-1]
    return pl.pallas_call(
        functools.partial(weight_kernel, sources_of, bits),
        in_specs=[pl.BlockSpec(memory_space=pl.ANY)] * (1 + len(inputs)),
        out_specs=[pl.BlockSpec(memory_space=pl.ANY)] * 2,
        out_shape=[
            jax.ShapeDtypeStruct((rows // halves, columns), F32),
            jax.ShapeDtypeStruct((halves - 1, rows // halves, columns), BF16),
        ],
        scratch_shapes=[
            pltpu.VMEM((rows, columns), F32),
            pltpu.VMEM(turned.shape, BF16),
            pltpu.VMEM((sources, tokens, columns), BF16),
            pltpu.VMEM((rows // halves, columns), F32),
            pltpu.VMEM((halves - 1, rows // halves, columns), BF16),
            pltpu.SemaphoreType.DMA((len(inputs) + 1,)),
            pltpu.SemaphoreType.DMA((2, max(columns // 512, 1))),
        ],
        compiler_params=pltpu.CompilerParams(vmem_limit_bytes=VMEM_MIB * 1024 * 1024),
        cost_estimate=pl.CostEstimate(
            flops=2 * sources * tokens * rows * columns,
            bytes_accessed=sources * tokens * columns * 2 + rows * columns * 6,
            transcendentals=0,
        ),
    )(turned, *inputs)


def shards(layer_input, query_rows, key_rows, value_rows, out_grad, bits):
    query, key, value, upstream = query_rows[0], key_rows[0], value_rows[0], out_grad[0]
    tokens, features = query.shape
    sequences = lax.axis_size("dp")
    places = 2 ** len(bits)
    core, side, layer, *high = bits
    spans = tuple(reversed(high))
    halves = places // 8
    cuts = 2
    rows = features // places // cuts

    (block_state,) = by_heads(
        block_state_head, [("row", key), ("row", value)], [("held state", BF16)], 1, vmem=44
    )
    forward = Scan(block_state, bits, False)

    if sequences == 2:
        own, gone = sides(after(layer_input[0], forward.mine))
        own, far = own[None], swap(gone, "dp")[None]
    else:
        wide = lax.all_to_all(layer_input[0].reshape(tokens, sequences, -1), "dp", 1, 0)
        own, far = wide[: sequences // 2], wide[sequences // 2 :]

    far_side, far_both, output = [], [], []

    def along_side(token):
        far_side.append(swap(after(far, token), side))
        output.extend(
            by_heads(
                local_output_head,
                [("held", after(query, token)), ("held", key), ("held", value)],
                [("held row", F32)],
                2,
            )
        )
        return far_side + output

    forward.spread([], [far], along_side, True)
    forward.collect()
    far_layer = swap(after(far, forward.before), layer)
    grad_output, block_grad, state_in = by_heads(
        functools.partial(grad_output_head, forward.counts),
        [("held", query), ("held", output[0]), ("held", upstream), *forward.operands],
        [("held row", BF16), ("held state", BF16), ("state", BF16)],
        2,
        bits,
    )
    own_layer = swap(after(own, block_grad), layer)
    backward = Scan(after(block_grad, far_layer), bits, True)
    own_side = swap(after(own, backward.mine), side)
    (key_local,) = by_heads(
        key_local_head,
        [("held", query), ("held", value), ("held", after(grad_output, backward.mine))],
        [("held row", F32)],
        2,
    )

    def along_side_again(token):
        far_both.append(swap(after(far_layer, token), side))
        return far_both

    backward.spread([key_local], [own_side, own_layer], along_side_again, False)
    backward.collect()
    own_both = swap(after(own_side, backward.before), layer)
    key_grad, *turned = by_heads(
        functools.partial(key_grad_head, backward.counts),
        [("held", after(key, own_both)), ("held", value), ("held", key_local), *backward.operands],
        [("row", BF16)] + [((sequences, 8, halves, rows, tokens), BF16)] * cuts,
        1,
        bits,
    )
    own_ids, far_ids = range(sequences // 2), range(sequences // 2, sequences)
    held, sources_of = [], []
    for array, ids, layered, sided in (
        (own, own_ids, 0, 0),
        (far, far_ids, 0, 0),
        (own_layer, own_ids, 1, 0),
        (far_layer, far_ids, 1, 0),
        (far_side[0], far_ids, 0, 1),
        (far_both[0], far_ids, 1, 1),
        (own_side, own_ids, 0, 1),
        (own_both, own_ids, 1, 1),
    ):
        held.append(array)
        sources_of.append((ids, (0, sided, layered)))
    held += [swap(array, core) for array in held]
    sources_of += [(ids, (1, sided, layered)) for ids, (_, sided, layered) in sources_of]
    turned[0] = after(turned[0], *held[8:])

    sums, done = [], turned[0]
    for cut in range(cuts):
        part = turned[cut].reshape(sequences * 8, halves * rows, tokens)
        part = lax.all_to_all(part, ("dp", layer, side, core), 0, 0, tiled=True)
        total, sent = weight_part(sources_of, bits, after(part, done), held, halves)
        for turn in range(1, halves):
            moved = lax.ppermute(sent[turn - 1], spans, [(i, (i + turn) % halves) for i in range(halves)])
            total += moved.astype(F32)
        done = sent
        sums.append(total)
    weight_grad = jnp.concatenate(sums) * (sequences * places * tokens) ** (-0.5)
    query_grad, value_grad = by_heads(
        functools.partial(other_grads_head, backward.counts),
        [
            ("held", query),
            ("held", key),
            ("held", value),
            ("held", after(grad_output, done)),
            ("state", state_in),
            *backward.operands,
        ],
        [("row", BF16), ("row", BF16)],
        6,
        bits,
    )
    return (query_grad[None], key_grad[None], value_grad[None], weight_grad)


def solution(mesh):
    sequences, places = mesh.shape["dp"], mesh.shape["ctx"]
    bits = tuple(f"bit{i}" for i in range(places.bit_length() - 1))
    ctx = tuple(reversed(bits))
    devices = mesh.devices.reshape((sequences,) + (2,) * len(bits))
    rows = P("dp", ctx, None)
    return jax.shard_map(
        functools.partial(shards, bits=bits),
        mesh=jax.sharding.Mesh(devices, ("dp",) + ctx),
        in_specs=(rows,) * 5,
        out_specs=(rows, rows, rows, P(ctx, "dp")),
        check_vma=False,
    )
```

```python
import functools

import jax
import jax.numpy as jnp
from jax import lax
from jax.experimental import pallas as pl
from jax.experimental.pallas import tpu as pltpu
from jax.sharding import PartitionSpec as P

HEAD_DIM = 128
EPSILON = 1e-05
VMEM_MIB = 56
F32 = jnp.float32
BF16 = jnp.bfloat16

NN = (((1,), (0,)), ((), ()))
NT = (((1,), (1,)), ((), ()))
TN = (((0,), (0,)), ((), ()))


def dot(a, b, dims):
    return lax.dot_general(a, b, dims, preferred_element_type=F32)


def slope(values):
    wide = values.astype(F32)
    return jnp.where(wide > 0, 1.0, jnp.exp(jnp.minimum(wide, 0.0)))


def feature(values):
    wide = values.astype(F32)
    return jnp.where(wide > 0, wide + 1.0, jnp.exp(jnp.minimum(wide, 0.0))).astype(BF16)


def causal_scores(rows, columns):
    scores = dot(rows, columns, NT)
    t = lax.broadcasted_iota(jnp.int32, scores.shape, 0)
    s = lax.broadcasted_iota(jnp.int32, scores.shape, 1)
    return jnp.where(s <= t, scores, 0.0).astype(BF16)


def causal_scores_turned(rows, columns):
    scores = dot(columns, rows, NT)
    s = lax.broadcasted_iota(jnp.int32, scores.shape, 0)
    t = lax.broadcasted_iota(jnp.int32, scores.shape, 1)
    return jnp.where(s <= t, scores, 0.0).astype(BF16)


def block_state_head(at, k_ref, v_ref, state_ref):
    state_ref[at, :] = dot(feature(k_ref[:, at]), v_ref[:, at], TN).astype(BF16)


def local_output_head(at, q_ref, k_ref, v_ref, local_ref):
    scores = causal_scores(feature(q_ref[:, at]), feature(k_ref[:, at]))
    local_ref[:, at] = dot(scores, v_ref[:, at], NN)


def assemble(at, counts, flags_ref, other_ref, quarter_refs):
    size = quarter_refs[0].shape[0]
    quarter, start = divmod(at.start, size)
    near = flags_ref[0] == quarter // 2
    same = flags_ref[1] == quarter % 2
    own, other, swapped_own, swapped_other = [ref[start : start + HEAD_DIM, :] for ref in quarter_refs]
    total = jnp.where(same, jnp.where(near, own, swapped_own), jnp.where(near, other, swapped_other))
    return added_if(flags_ref[counts] == 1, total, other_ref[at, :])


def grad_output_head(counts, at, flags_ref, q_ref, local_ref, upstream_ref, other_ref, *refs):
    *quarter_refs, grad_ref, block_ref, state_ref = refs
    state = assemble(at, counts, flags_ref, other_ref, quarter_refs)
    state_ref[at, :] = state
    query = feature(q_ref[:, at])
    output = local_ref[:, at] + dot(query, state, NN)
    inverse_rms = lax.rsqrt(jnp.mean(output * output, axis=-1, keepdims=True) + EPSILON)
    normed = output * inverse_rms
    upstream = upstream_ref[:, at].astype(F32)
    projection = jnp.mean(upstream * normed, axis=-1, keepdims=True)
    grad = (inverse_rms * (upstream - normed * projection)).astype(BF16)
    grad_ref[:, at] = grad
    block_ref[at, :] = dot(query, grad, TN).astype(BF16)


def key_local_head(at, q_ref, v_ref, grad_ref, key_out):
    grad_scores = causal_scores_turned(grad_ref[:, at], v_ref[:, at])
    key_out[:, at] = dot(grad_scores, feature(q_ref[:, at]), NN)


def key_grad_head(counts, at, flags_ref, k_ref, v_ref, local_ref, other_ref, *refs):
    *quarter_refs, key_out = refs[:5]
    turned_out = refs[5:]
    cuts = len(turned_out)
    copies, devices, halves, rows, tokens = turned_out[0].shape
    state = assemble(at, counts, flags_ref, other_ref, quarter_refs)
    key = local_ref[:, at] + dot(v_ref[:, at], state, NT)
    key = (key * slope(k_ref[:, at])).astype(BF16)
    key_out[:, at] = key
    turned = key.T
    start = at.start
    while start < at.stop:
        block, row = divmod(start, rows)
        size = min(rows - row, at.stop - start)
        owner, cut = divmod(block, cuts)
        half, device = divmod(owner, devices)
        for copy in range(copies):
            turned_out[cut][copy, device, half, row : row + size] = turned[start - at.start : start - at.start + size]
        start += size


def other_grads_head(counts, at, flags_ref, q_ref, k_ref, v_ref, grad_ref, state_ref, other_ref, *refs):
    *quarter_refs, query_out, value_out = refs
    later = assemble(at, counts, flags_ref, other_ref, quarter_refs)
    grad = grad_ref[:, at]
    key = feature(k_ref[:, at])
    grad_scores = causal_scores(grad, v_ref[:, at])
    query = dot(grad_scores, key, NN) + dot(grad, state_ref[at, :], NT)
    query_out[:, at] = (query * slope(q_ref[:, at])).astype(BF16)
    scores = causal_scores_turned(feature(q_ref[:, at]), key)
    value = dot(scores, grad, NN) + dot(key, later, NN)
    value_out[:, at] = value.astype(BF16)


def by_heads(head, operands, outs, matmuls, bits=None, vmem=12):
    tokens, features = operands[0][1].shape
    groups = 2 if features % (2 * HEAD_DIM) == 0 else 1
    group = features // groups
    shapes = {"row": (tokens, features), "state": (features, HEAD_DIM)}
    shapes_held = {"held row": shapes["row"], "held state": shapes["state"]}
    kinds = [kind for kind, _ in operands] + [kind for kind, _ in outs]
    results = [
        jax.ShapeDtypeStruct(shapes.get(kind) or shapes_held.get(kind, kind), dtype) for kind, dtype in outs
    ]
    held = [kind == "held" or kind in shapes_held for kind in kinds]
    arrays = [array for _, array in operands] + results
    count = len(operands)

    def part(kind, ref, index):
        cut = pl.ds(index * group, group)
        return ref.at[:, cut] if kind == "row" else ref.at[cut, :]

    def body(*refs):
        numbers = [] if bits is None else [numbers_of(bits)]
        there, moved = refs[: len(kinds)], refs[-1]
        scratch = iter(refs[len(kinds) : -1])
        here = [ref if stays else next(scratch) for stays, ref in zip(held, there)]

        def copy(index, step):
            source, target = (there, here) if index < count else (here, there)
            source, target = source[index], target[index]
            if kinds[index] in shapes:
                source, target = part(kinds[index], source, step), part(kinds[index], target, step)
            return pltpu.make_async_copy(source, target, moved.at[index, step])

        def at_once(index, step):
            return step == (0 if index < count else groups - 1)

        def due(step, indices):
            moving = [index for index in indices if not held[index]]
            return [index for index in moving if kinds[index] in shapes or at_once(index, step)]

        ins, outputs = range(count), range(count, len(kinds))
        for step in range(groups):
            for index in due(step, ins):
                copy(index, step).start()
        for step in range(groups):
            for index in due(step, ins):
                copy(index, step).wait()
            for start in range(step * group, (step + 1) * group, HEAD_DIM):
                head(slice(start, start + HEAD_DIM), *numbers, *here)
            for index in due(step, outputs):
                copy(index, step).start()
        for step in range(groups):
            for index in due(step, outputs):
                copy(index, step).wait()

    anywhere = pl.BlockSpec(memory_space=pl.ANY)
    places = [pl.BlockSpec(memory_space=pltpu.VMEM) if stays else anywhere for stays in held]
    return pl.pallas_call(
        body,
        in_specs=places[:count],
        out_specs=places[count:],
        out_shape=results,
        scratch_shapes=[
            pltpu.VMEM(array.shape, array.dtype) for stays, array in zip(held, arrays) if not stays
        ]
        + [pltpu.SemaphoreType.DMA((len(kinds), groups))],
        compiler_params=pltpu.CompilerParams(vmem_limit_bytes=vmem * 1024 * 1024),
        cost_estimate=pl.CostEstimate(
            flops=2 * matmuls * tokens * features * HEAD_DIM,
            bytes_accessed=tokens * features * 2 * len(kinds),
            transcendentals=0,
        ),
    )(*[array for _, array in operands])


def swap(array, axis):
    return lax.ppermute(array, axis, [(0, 1), (1, 0)])


def numbers_of(bits):
    place = [lax.axis_index(bit) for bit in bits]
    span = sum(2**index * at for index, at in enumerate(place[3:]))
    return place + place + [1 - at for at in place] + [lax.axis_index("dp"), span]


def added_if(flag, a, b):
    return (a.astype(F32) + jnp.where(flag, b.astype(F32), 0.0)).astype(BF16)


def small(body, bits, arrays, outs):
    vmem = pl.BlockSpec(memory_space=pltpu.VMEM)
    result = jax.ShapeDtypeStruct(arrays[-1].shape[-2:], BF16)

    def kernel(*refs):
        values = body(numbers_of(bits), *refs[: len(arrays)])
        for ref, value in zip(refs[len(arrays) :], values):
            ref[...] = value

    return pl.pallas_call(
        kernel,
        in_specs=[vmem] * len(arrays),
        out_specs=[vmem] * outs,
        out_shape=[result] * outs,
        compiler_params=pltpu.CompilerParams(vmem_limit_bytes=4 * 1024 * 1024),
        cost_estimate=pl.CostEstimate(flops=0, bytes_accessed=1024, transcendentals=0),
    )(*arrays)


def after(array, *others):
    if not others:
        return array
    return lax.optimization_barrier((array,) + others)[0]


class Scan:
    def __init__(self, state, bits, backward):
        first, second, *self.rest = bits
        self.first, self.second = first, second
        self.bits, self.counts = bits, (2 if backward else 1) * len(bits)
        state = state.reshape(2, 2, -1, HEAD_DIM)
        self.other = swap(state, first)

        def quarters(flags, state, other):
            core, side = flags[0], flags[1]
            return [added_if(True, state[core, at], other[core, at]) for at in (1 - side, side)]

        self.theirs, self.mine = small(quarters, self.bits, [state, self.other], 2)
        self.arrived = swap(self.theirs, second)

    def spread(self, due, early, meanwhile, rest_early):
        counts = self.counts
        self.arrived = after(self.arrived, *due)

        def start(flags, mine, arrived):
            return [added_if(True, mine[...], arrived[...])]

        (total,) = small(start, self.bits, [self.mine, self.arrived], 1)
        self.rest_arrived = swap(after(self.mine, self.arrived), self.second)
        if rest_early:
            early = [self.rest_arrived, *early]
        before = None
        for index, bit in enumerate(self.rest, 2):
            last = bit == self.rest[-1]
            pieces = meanwhile(total) if last else list(early)
            arrived = after(swap(total, bit), *pieces)

            def first(flags, total, arrived):
                values = arrived[...], total[...]
                return [jnp.where(flags[counts + 2] == 1, values[0], 0.0), added_if(True, *values)]

            def middle(flags, total, arrived, before):
                value = added_if(flags[counts + index] == 1, before[...], arrived[...])
                return [value, added_if(True, total[...], arrived[...])]

            def final(flags, side, arrived, before):
                value = added_if(flags[counts + index] == 1, before[...], arrived[...])
                return [value, added_if(flags[counts + 1] == 1, value, side[...])]

            if before is None:
                before, total = small(first, self.bits, [total, arrived], 2)
            elif not last:
                before, total = small(middle, self.bits, [total, arrived, before], 2)
            else:
                self.before, self.own = small(final, self.bits, [self.arrived, arrived, before], 2)

    def collect(self):
        counts = self.counts

        def finish(flags, swapped, rest):
            return [added_if(flags[counts + 1] == 1, swapped[...], rest[...])]

        arrays = [swap(self.before, self.second), self.rest_arrived]
        (other,) = small(finish, self.bits, arrays, 1)
        quarters = [self.own, other, swap(self.own, self.first), swap(other, self.first)]
        self.operands = [("whole", self.other.reshape(-1, HEAD_DIM))]
        self.operands += [("held", quarter) for quarter in quarters]


def sides_kernel(in_ref, own_ref, gone_ref):
    columns = own_ref.shape[1]
    mine = lax.axis_index("dp")

    @pl.when(mine == 0)
    def _():
        own_ref[...] = in_ref[:, :columns]
        gone_ref[...] = in_ref[:, columns:]

    @pl.when(mine == 1)
    def _():
        own_ref[...] = in_ref[:, columns:]
        gone_ref[...] = in_ref[:, :columns]


def sides(array):
    rows, columns = array.shape
    tile = rows // 2
    out = jax.ShapeDtypeStruct((rows, columns // 2), array.dtype)
    return pl.pallas_call(
        sides_kernel,
        grid=(rows // tile,),
        in_specs=[pl.BlockSpec((tile, columns), lambda i: (i, 0))],
        out_specs=[pl.BlockSpec((tile, columns // 2), lambda i: (i, 0))] * 2,
        out_shape=[out, out],
        compiler_params=pltpu.CompilerParams(vmem_limit_bytes=VMEM_MIB * 1024 * 1024),
        cost_estimate=pl.CostEstimate(flops=0, bytes_accessed=4 * array.size, transcendentals=0),
    )(array)


def weight_kernel(sources_of, bits, turned_in, *refs):
    *numbers, mine, span = numbers_of(bits)
    order = []
    for sequences, flips in sources_of:
        device = 0
        for bit, flip in enumerate(flips):
            device += 2**bit * (1 - numbers[bit] if flip else numbers[bit])
        pair = turned_in.shape[0] == 16
        order += [8 * (lax.rem(mine + at, 2) if pair else at) + device for at in sequences]
    *held, kept_out, sent_out, total_ref, turned_ref, buffer_ref, kept_ref, sent_ref, arrival, departure = refs
    sources, _, tokens = turned_ref.shape
    others, rows, columns = sent_ref.shape
    turning = pltpu.make_async_copy(turned_in, turned_ref, arrival.at[len(held)])
    turning.start()
    copies, at = [], 0
    for index, ref in enumerate(held):
        count = ref.shape[0]
        copies.append(pltpu.make_async_copy(ref, buffer_ref.at[at : at + count], arrival.at[index]))
        copies[-1].start()
        at += count
    per_step, tile = 4, 512 if columns % 512 == 0 else columns
    steps = sources // per_step
    leaving = []
    turning.wait()
    for step in range(steps):
        for copy in copies[step * len(copies) // steps : (step + 1) * len(copies) // steps]:
            copy.wait()
        first = step * per_step
        lhs = jnp.concatenate([turned_ref[order[first + i]] for i in range(per_step)], axis=1)
        for index, start in enumerate(range(0, columns, tile)):
            cut = slice(start, start + tile)
            rhs = buffer_ref[first : first + per_step, :, cut].reshape(per_step * tokens, tile)
            product = dot(lhs, rhs, NN)
            total_ref[:, cut] = product if step == 0 else total_ref[:, cut] + product
            if step < steps - 1:
                continue
            kept_ref[:, cut] = total_ref[pl.ds(pl.multiple_of(span * rows, 16), rows), cut]
            for turn in range(others):
                target = lax.rem(span + turn + 1, others + 1)
                sent_ref[turn, :, cut] = total_ref[pl.ds(pl.multiple_of(target * rows, 16), rows), cut].astype(BF16)
            there = pl.ds(start, tile)
            leaving += [
                pltpu.make_async_copy(kept_ref.at[:, there], kept_out.at[:, there], departure.at[0, index]),
                pltpu.make_async_copy(sent_ref.at[:, :, there], sent_out.at[:, :, there], departure.at[1, index]),
            ]
            leaving[-2].start()
            leaving[-1].start()
    for copy in leaving:
        copy.wait()


def weight_part(sources_of, bits, turned, inputs, halves):
    sources, rows, tokens = turned.shape
    columns = inputs[0].shape[-1]
    return pl.pallas_call(
        functools.partial(weight_kernel, sources_of, bits),
        in_specs=[pl.BlockSpec(memory_space=pl.ANY)] * (1 + len(inputs)),
        out_specs=[pl.BlockSpec(memory_space=pl.ANY)] * 2,
        out_shape=[
            jax.ShapeDtypeStruct((rows // halves, columns), F32),
            jax.ShapeDtypeStruct((halves - 1, rows // halves, columns), BF16),
        ],
        scratch_shapes=[
            pltpu.VMEM((rows, columns), F32),
            pltpu.VMEM(turned.shape, BF16),
            pltpu.VMEM((sources, tokens, columns), BF16),
            pltpu.VMEM((rows // halves, columns), F32),
            pltpu.VMEM((halves - 1, rows // halves, columns), BF16),
            pltpu.SemaphoreType.DMA((len(inputs) + 1,)),
            pltpu.SemaphoreType.DMA((2, max(columns // 512, 1))),
        ],
        compiler_params=pltpu.CompilerParams(vmem_limit_bytes=VMEM_MIB * 1024 * 1024),
        cost_estimate=pl.CostEstimate(
            flops=2 * sources * tokens * rows * columns,
            bytes_accessed=sources * tokens * columns * 2 + rows * columns * 6,
            transcendentals=0,
        ),
    )(turned, *inputs)


def shards(layer_input, query_rows, key_rows, value_rows, out_grad, bits):
    query, key, value, upstream = query_rows[0], key_rows[0], value_rows[0], out_grad[0]
    tokens, features = query.shape
    sequences = lax.axis_size("dp")
    places = 2 ** len(bits)
    core, side, layer, *high = bits
    spans = tuple(reversed(high))
    halves = places // 8
    cuts = 2
    rows = features // places // cuts

    (block_state,) = by_heads(
        block_state_head, [("held", key), ("held", value)], [("held state", BF16)], 1
    )
    forward = Scan(block_state, bits, False)

    if sequences == 2:
        own, gone = sides(after(layer_input[0], forward.mine))
        own, far = own[None], swap(gone, "dp")[None]
    else:
        wide = lax.all_to_all(layer_input[0].reshape(tokens, sequences, -1), "dp", 1, 0)
        own, far = wide[: sequences // 2], wide[sequences // 2 :]

    far_side, far_both, output = [], [], []

    def along_side(token):
        far_side.append(swap(after(far, token), side))
        output.extend(
            by_heads(
                local_output_head,
                [("held", after(query, token)), ("held", key), ("held", value)],
                [("held row", F32)],
                2,
            )
        )
        return far_side + output

    forward.spread([], [far], along_side, True)
    forward.collect()
    far_layer = swap(after(far, forward.before), layer)
    grad_output, block_grad, state_in = by_heads(
        functools.partial(grad_output_head, forward.counts),
        [("held", query), ("held", output[0]), ("held", upstream), *forward.operands],
        [("held row", BF16), ("held state", BF16), ("state", BF16)],
        2,
        bits,
    )
    own_layer = swap(after(own, block_grad), layer)
    backward = Scan(after(block_grad, far_layer), bits, True)
    own_side = swap(after(own, backward.mine), side)
    (key_local,) = by_heads(
        key_local_head,
        [("held", query), ("held", value), ("held", after(grad_output, backward.mine))],
        [("held row", F32)],
        2,
    )

    def along_side_again(token):
        far_both.append(swap(after(far_layer, token), side))
        return far_both

    backward.spread([key_local], [own_side, own_layer], along_side_again, False)
    backward.collect()
    own_both = swap(after(own_side, backward.before), layer)
    key_grad, *turned = by_heads(
        functools.partial(key_grad_head, backward.counts),
        [("held", after(key, own_both)), ("held", value), ("held", key_local), *backward.operands],
        [("row", BF16)] + [((sequences, 8, halves, rows, tokens), BF16)] * cuts,
        1,
        bits,
    )
    own_ids, far_ids = range(sequences // 2), range(sequences // 2, sequences)
    held, sources_of = [], []
    for array, ids, layered, sided in (
        (own, own_ids, 0, 0),
        (far, far_ids, 0, 0),
        (own_layer, own_ids, 1, 0),
        (far_layer, far_ids, 1, 0),
        (far_side[0], far_ids, 0, 1),
        (far_both[0], far_ids, 1, 1),
        (own_side, own_ids, 0, 1),
        (own_both, own_ids, 1, 1),
    ):
        held.append(array)
        sources_of.append((ids, (0, sided, layered)))
    held += [swap(array, core) for array in held]
    sources_of += [(ids, (1, sided, layered)) for ids, (_, sided, layered) in sources_of]
    turned[0] = after(turned[0], *held[8:])

    sums, done = [], turned[0]
    for cut in range(cuts):
        part = turned[cut].reshape(sequences * 8, halves * rows, tokens)
        part = lax.all_to_all(part, ("dp", layer, side, core), 0, 0, tiled=True)
        total, sent = weight_part(sources_of, bits, after(part, done), held, halves)
        for turn in range(1, halves):
            moved = lax.ppermute(sent[turn - 1], spans, [(i, (i + turn) % halves) for i in range(halves)])
            total += moved.astype(F32)
        done = sent
        sums.append(total)
    weight_grad = jnp.concatenate(sums) * (sequences * places * tokens) ** (-0.5)
    query_grad, value_grad = by_heads(
        functools.partial(other_grads_head, backward.counts),
        [
            ("held", query),
            ("held", key),
            ("held", value),
            ("held", after(grad_output, done)),
            ("state", state_in),
            *backward.operands,
        ],
        [("row", BF16), ("row", BF16)],
        6,
        bits,
    )
    return (query_grad[None], key_grad[None], value_grad[None], weight_grad)


def solution(mesh):
    sequences, places = mesh.shape["dp"], mesh.shape["ctx"]
    bits = tuple(f"bit{i}" for i in range(places.bit_length() - 1))
    ctx = tuple(reversed(bits))
    devices = mesh.devices.reshape((sequences,) + (2,) * len(bits))
    rows = P("dp", ctx, None)
    return jax.shard_map(
        functools.partial(shards, bits=bits),
        mesh=jax.sharding.Mesh(devices, ("dp",) + ctx),
        in_specs=(rows,) * 5,
        out_specs=(rows, rows, rows, P(ctx, "dp")),
        check_vma=False,
    )
```

```python
import functools

import jax
import jax.numpy as jnp
from jax import lax
from jax.experimental import pallas as pl
from jax.experimental.pallas import tpu as pltpu
from jax.sharding import PartitionSpec as P

HEAD_DIM = 128
EPSILON = 1e-05
VMEM_MIB = 56
F32 = jnp.float32
BF16 = jnp.bfloat16

NN = (((1,), (0,)), ((), ()))
NT = (((1,), (1,)), ((), ()))
TN = (((0,), (0,)), ((), ()))


def dot(a, b, dims):
    return lax.dot_general(a, b, dims, preferred_element_type=F32)


def slope(values):
    wide = values.astype(F32)
    return jnp.where(wide > 0, 1.0, jnp.exp(jnp.minimum(wide, 0.0)))


def feature(values):
    wide = values.astype(F32)
    return jnp.where(wide > 0, wide + 1.0, jnp.exp(jnp.minimum(wide, 0.0))).astype(BF16)


def causal_scores(rows, columns):
    scores = dot(rows, columns, NT)
    t = lax.broadcasted_iota(jnp.int32, scores.shape, 0)
    s = lax.broadcasted_iota(jnp.int32, scores.shape, 1)
    return jnp.where(s <= t, scores, 0.0).astype(BF16)


def causal_scores_turned(rows, columns):
    scores = dot(columns, rows, NT)
    s = lax.broadcasted_iota(jnp.int32, scores.shape, 0)
    t = lax.broadcasted_iota(jnp.int32, scores.shape, 1)
    return jnp.where(s <= t, scores, 0.0).astype(BF16)


def block_state_head(at, k_ref, v_ref, state_ref):
    state_ref[at, :] = dot(feature(k_ref[:, at]), v_ref[:, at], TN).astype(BF16)


def local_output_head(at, q_ref, k_ref, v_ref, local_ref):
    scores = causal_scores(feature(q_ref[:, at]), feature(k_ref[:, at]))
    local_ref[:, at] = dot(scores, v_ref[:, at], NN)


def assemble(at, counts, flags_ref, other_ref, quarter_refs):
    size = quarter_refs[0].shape[0]
    quarter, start = divmod(at.start, size)
    near = flags_ref[0] == quarter // 2
    same = flags_ref[1] == quarter % 2
    own, other, swapped_own, swapped_other = [ref[start : start + HEAD_DIM, :] for ref in quarter_refs]
    total = jnp.where(same, jnp.where(near, own, swapped_own), jnp.where(near, other, swapped_other))
    return added_if(flags_ref[counts] == 1, total, other_ref[at, :])


def grad_output_head(counts, at, flags_ref, q_ref, local_ref, upstream_ref, other_ref, *refs):
    *quarter_refs, grad_ref, block_ref, state_ref = refs
    state = assemble(at, counts, flags_ref, other_ref, quarter_refs)
    state_ref[at, :] = state
    query = feature(q_ref[:, at])
    output = local_ref[:, at] + dot(query, state, NN)
    inverse_rms = lax.rsqrt(jnp.mean(output * output, axis=-1, keepdims=True) + EPSILON)
    normed = output * inverse_rms
    upstream = upstream_ref[:, at].astype(F32)
    projection = jnp.mean(upstream * normed, axis=-1, keepdims=True)
    grad = (inverse_rms * (upstream - normed * projection)).astype(BF16)
    grad_ref[:, at] = grad
    block_ref[at, :] = dot(query, grad, TN).astype(BF16)


def key_local_head(at, q_ref, v_ref, grad_ref, key_out):
    grad_scores = causal_scores_turned(grad_ref[:, at], v_ref[:, at])
    key_out[:, at] = dot(grad_scores, feature(q_ref[:, at]), NN)


def key_grad_head(counts, at, flags_ref, k_ref, v_ref, local_ref, other_ref, *refs):
    *quarter_refs, key_out = refs[:5]
    turned_out = refs[5:]
    cuts = len(turned_out)
    copies, devices, halves, rows, tokens = turned_out[0].shape
    state = assemble(at, counts, flags_ref, other_ref, quarter_refs)
    key = local_ref[:, at] + dot(v_ref[:, at], state, NT)
    key = (key * slope(k_ref[:, at])).astype(BF16)
    key_out[:, at] = key
    turned = key.T
    start = at.start
    while start < at.stop:
        block, row = divmod(start, rows)
        size = min(rows - row, at.stop - start)
        owner, cut = divmod(block, cuts)
        half, device = divmod(owner, devices)
        for copy in range(copies):
            turned_out[cut][copy, device, half, row : row + size] = turned[start - at.start : start - at.start + size]
        start += size


def other_grads_head(counts, at, flags_ref, q_ref, k_ref, v_ref, grad_ref, state_ref, other_ref, *refs):
    *quarter_refs, query_out, value_out = refs
    later = assemble(at, counts, flags_ref, other_ref, quarter_refs)
    grad = grad_ref[:, at]
    key = feature(k_ref[:, at])
    grad_scores = causal_scores(grad, v_ref[:, at])
    query = dot(grad_scores, key, NN) + dot(grad, state_ref[at, :], NT)
    query_out[:, at] = (query * slope(q_ref[:, at])).astype(BF16)
    scores = causal_scores_turned(feature(q_ref[:, at]), key)
    value = dot(scores, grad, NN) + dot(key, later, NN)
    value_out[:, at] = value.astype(BF16)


def by_heads(head, operands, outs, matmuls, bits=None, vmem=12):
    tokens, features = operands[0][1].shape
    groups = 2 if features % (2 * HEAD_DIM) == 0 else 1
    group = features // groups
    shapes = {"row": (tokens, features), "state": (features, HEAD_DIM)}
    shapes_held = {"held row": shapes["row"], "held state": shapes["state"]}
    kinds = [kind for kind, _ in operands] + [kind for kind, _ in outs]
    results = [
        jax.ShapeDtypeStruct(shapes.get(kind) or shapes_held.get(kind, kind), dtype) for kind, dtype in outs
    ]
    held = [kind == "held" or kind in shapes_held for kind in kinds]
    arrays = [array for _, array in operands] + results
    count = len(operands)

    def part(kind, ref, index):
        cut = pl.ds(index * group, group)
        return ref.at[:, cut] if kind == "row" else ref.at[cut, :]

    def body(*refs):
        numbers = [] if bits is None else [numbers_of(bits)]
        there, moved = refs[: len(kinds)], refs[-1]
        scratch = iter(refs[len(kinds) : -1])
        here = [ref if stays else next(scratch) for stays, ref in zip(held, there)]

        def copy(index, step):
            source, target = (there, here) if index < count else (here, there)
            source, target = source[index], target[index]
            if kinds[index] in shapes:
                source, target = part(kinds[index], source, step), part(kinds[index], target, step)
            return pltpu.make_async_copy(source, target, moved.at[index, step])

        def at_once(index, step):
            return step == (0 if index < count else groups - 1)

        def due(step, indices):
            moving = [index for index in indices if not held[index]]
            return [index for index in moving if kinds[index] in shapes or at_once(index, step)]

        ins, outputs = range(count), range(count, len(kinds))
        for step in range(groups):
            for index in due(step, ins):
                copy(index, step).start()
        for step in range(groups):
            for index in due(step, ins):
                copy(index, step).wait()
            for start in range(step * group, (step + 1) * group, HEAD_DIM):
                head(slice(start, start + HEAD_DIM), *numbers, *here)
            for index in due(step, outputs):
                copy(index, step).start()
        for step in range(groups):
            for index in due(step, outputs):
                copy(index, step).wait()

    anywhere = pl.BlockSpec(memory_space=pl.ANY)
    places = [pl.BlockSpec(memory_space=pltpu.VMEM) if stays else anywhere for stays in held]
    return pl.pallas_call(
        body,
        in_specs=places[:count],
        out_specs=places[count:],
        out_shape=results,
        scratch_shapes=[
            pltpu.VMEM(array.shape, array.dtype) for stays, array in zip(held, arrays) if not stays
        ]
        + [pltpu.SemaphoreType.DMA((len(kinds), groups))],
        compiler_params=pltpu.CompilerParams(vmem_limit_bytes=vmem * 1024 * 1024),
        cost_estimate=pl.CostEstimate(
            flops=2 * matmuls * tokens * features * HEAD_DIM,
            bytes_accessed=tokens * features * 2 * len(kinds),
            transcendentals=0,
        ),
    )(*[array for _, array in operands])


def swap(array, axis):
    return lax.ppermute(array, axis, [(0, 1), (1, 0)])


def numbers_of(bits):
    place = [lax.axis_index(bit) for bit in bits]
    span = sum(2**index * at for index, at in enumerate(place[3:]))
    return place + place + [1 - at for at in place] + [lax.axis_index("dp"), span]


def added_if(flag, a, b):
    return (a.astype(F32) + jnp.where(flag, b.astype(F32), 0.0)).astype(BF16)


def small(body, bits, arrays, outs):
    vmem = pl.BlockSpec(memory_space=pltpu.VMEM)
    result = jax.ShapeDtypeStruct(arrays[-1].shape[-2:], BF16)

    def kernel(*refs):
        values = body(numbers_of(bits), *refs[: len(arrays)])
        for ref, value in zip(refs[len(arrays) :], values):
            ref[...] = value

    return pl.pallas_call(
        kernel,
        in_specs=[vmem] * len(arrays),
        out_specs=[vmem] * outs,
        out_shape=[result] * outs,
        compiler_params=pltpu.CompilerParams(vmem_limit_bytes=4 * 1024 * 1024),
        cost_estimate=pl.CostEstimate(flops=0, bytes_accessed=1024, transcendentals=0),
    )(*arrays)


def after(array, *others):
    if not others:
        return array
    return lax.optimization_barrier((array,) + others)[0]


class Scan:
    def __init__(self, state, bits, backward):
        first, second, *self.rest = bits
        self.first, self.second = first, second
        self.bits, self.counts = bits, (2 if backward else 1) * len(bits)
        state = state.reshape(2, 2, -1, HEAD_DIM)
        self.other = swap(state, first)

        def quarters(flags, state, other):
            core, side = flags[0], flags[1]
            return [added_if(True, state[core, at], other[core, at]) for at in (1 - side, side)]

        self.theirs, self.mine = small(quarters, self.bits, [state, self.other], 2)
        self.arrived = swap(self.theirs, second)

    def spread(self, due, early, meanwhile, rest_early):
        counts = self.counts
        self.arrived = after(self.arrived, *due)

        def start(flags, mine, arrived):
            return [added_if(True, mine[...], arrived[...])]

        (total,) = small(start, self.bits, [self.mine, self.arrived], 1)
        self.rest_arrived = swap(after(self.mine, self.arrived), self.second)
        if rest_early:
            early = [self.rest_arrived, *early]
        before = None
        for index, bit in enumerate(self.rest, 2):
            last = bit == self.rest[-1]
            pieces = meanwhile(total) if last else list(early)
            arrived = after(swap(total, bit), *pieces)

            def first(flags, total, arrived):
                values = arrived[...], total[...]
                return [jnp.where(flags[counts + 2] == 1, values[0], 0.0), added_if(True, *values)]

            def middle(flags, total, arrived, before):
                value = added_if(flags[counts + index] == 1, before[...], arrived[...])
                return [value, added_if(True, total[...], arrived[...])]

            def final(flags, side, arrived, before):
                value = added_if(flags[counts + index] == 1, before[...], arrived[...])
                return [value, added_if(flags[counts + 1] == 1, value, side[...])]

            if before is None:
                before, total = small(first, self.bits, [total, arrived], 2)
            elif not last:
                before, total = small(middle, self.bits, [total, arrived, before], 2)
            else:
                self.before, self.own = small(final, self.bits, [self.arrived, arrived, before], 2)

    def collect(self):
        counts = self.counts

        def finish(flags, swapped, rest):
            return [added_if(flags[counts + 1] == 1, swapped[...], rest[...])]

        arrays = [swap(self.before, self.second), self.rest_arrived]
        (other,) = small(finish, self.bits, arrays, 1)
        quarters = [self.own, other, swap(self.own, self.first), swap(other, self.first)]
        self.operands = [("whole", self.other.reshape(-1, HEAD_DIM))]
        self.operands += [("held", quarter) for quarter in quarters]


def sides_kernel(in_ref, own_ref, gone_ref):
    columns = own_ref.shape[1]
    mine = lax.axis_index("dp")

    @pl.when(mine == 0)
    def _():
        own_ref[...] = in_ref[:, :columns]
        gone_ref[...] = in_ref[:, columns:]

    @pl.when(mine == 1)
    def _():
        own_ref[...] = in_ref[:, columns:]
        gone_ref[...] = in_ref[:, :columns]


def sides(array):
    rows, columns = array.shape
    tile = rows // 2
    out = jax.ShapeDtypeStruct((rows, columns // 2), array.dtype)
    return pl.pallas_call(
        sides_kernel,
        grid=(rows // tile,),
        in_specs=[pl.BlockSpec((tile, columns), lambda i: (i, 0))],
        out_specs=[pl.BlockSpec((tile, columns // 2), lambda i: (i, 0))] * 2,
        out_shape=[out, out],
        compiler_params=pltpu.CompilerParams(vmem_limit_bytes=VMEM_MIB * 1024 * 1024),
        cost_estimate=pl.CostEstimate(flops=0, bytes_accessed=4 * array.size, transcendentals=0),
    )(array)


def weight_kernel(sources_of, bits, turned_in, *refs):
    *numbers, mine, span = numbers_of(bits)
    order = []
    for sequences, flips in sources_of:
        device = 0
        for bit, flip in enumerate(flips):
            device += 2**bit * (1 - numbers[bit] if flip else numbers[bit])
        pair = turned_in.shape[0] == 16
        order += [8 * (lax.rem(mine + at, 2) if pair else at) + device for at in sequences]
    *held, kept_out, sent_out, total_ref, turned_ref, buffer_ref, kept_ref, sent_ref, arrival, departure = refs
    sources, _, tokens = turned_ref.shape
    others, rows, columns = sent_ref.shape
    turning = pltpu.make_async_copy(turned_in, turned_ref, arrival.at[len(held)])
    turning.start()
    copies, at = [], 0
    for index, ref in enumerate(held):
        count = ref.shape[0]
        copies.append(pltpu.make_async_copy(ref, buffer_ref.at[at : at + count], arrival.at[index]))
        copies[-1].start()
        at += count
    per_step, tile = 4, 512 if columns % 512 == 0 else columns
    steps = sources // per_step
    leaving = []
    turning.wait()
    for step in range(steps):
        for copy in copies[step * len(copies) // steps : (step + 1) * len(copies) // steps]:
            copy.wait()
        first = step * per_step
        lhs = jnp.concatenate([turned_ref[order[first + i]] for i in range(per_step)], axis=1)
        for index, start in enumerate(range(0, columns, tile)):
            cut = slice(start, start + tile)
            rhs = buffer_ref[first : first + per_step, :, cut].reshape(per_step * tokens, tile)
            product = dot(lhs, rhs, NN)
            total_ref[:, cut] = product if step == 0 else total_ref[:, cut] + product
            if step < steps - 1:
                continue
            kept_ref[:, cut] = total_ref[pl.ds(pl.multiple_of(span * rows, 16), rows), cut]
            for turn in range(others):
                target = lax.rem(span + turn + 1, others + 1)
                sent_ref[turn, :, cut] = total_ref[pl.ds(pl.multiple_of(target * rows, 16), rows), cut].astype(BF16)
            there = pl.ds(start, tile)
            leaving += [
                pltpu.make_async_copy(kept_ref.at[:, there], kept_out.at[:, there], departure.at[0, index]),
                pltpu.make_async_copy(sent_ref.at[:, :, there], sent_out.at[:, :, there], departure.at[1, index]),
            ]
            leaving[-2].start()
            leaving[-1].start()
    for copy in leaving:
        copy.wait()


def weight_part(sources_of, bits, turned, inputs, halves):
    sources, rows, tokens = turned.shape
    columns = inputs[0].shape[-1]
    return pl.pallas_call(
        functools.partial(weight_kernel, sources_of, bits),
        in_specs=[pl.BlockSpec(memory_space=pl.ANY)] * (1 + len(inputs)),
        out_specs=[pl.BlockSpec(memory_space=pl.ANY)] * 2,
        out_shape=[
            jax.ShapeDtypeStruct((rows // halves, columns), F32),
            jax.ShapeDtypeStruct((halves - 1, rows // halves, columns), BF16),
        ],
        scratch_shapes=[
            pltpu.VMEM((rows, columns), F32),
            pltpu.VMEM(turned.shape, BF16),
            pltpu.VMEM((sources, tokens, columns), BF16),
            pltpu.VMEM((rows // halves, columns), F32),
            pltpu.VMEM((halves - 1, rows // halves, columns), BF16),
            pltpu.SemaphoreType.DMA((len(inputs) + 1,)),
            pltpu.SemaphoreType.DMA((2, max(columns // 512, 1))),
        ],
        compiler_params=pltpu.CompilerParams(vmem_limit_bytes=VMEM_MIB * 1024 * 1024),
        cost_estimate=pl.CostEstimate(
            flops=2 * sources * tokens * rows * columns,
            bytes_accessed=sources * tokens * columns * 2 + rows * columns * 6,
            transcendentals=0,
        ),
    )(turned, *inputs)


def shards(layer_input, query_rows, key_rows, value_rows, out_grad, bits):
    query, key, value, upstream = query_rows[0], key_rows[0], value_rows[0], out_grad[0]
    tokens, features = query.shape
    sequences = lax.axis_size("dp")
    places = 2 ** len(bits)
    core, side, layer, *high = bits
    spans = tuple(reversed(high))
    halves = places // 8
    cuts = 2
    rows = features // places // cuts

    (block_state,) = by_heads(
        block_state_head, [("held", key), ("held", value)], [("held state", BF16)], 1
    )
    forward = Scan(block_state, bits, False)

    if sequences == 2:
        own, gone = sides(after(layer_input[0], forward.mine))
        own, far = own[None], swap(gone, "dp")[None]
    else:
        wide = lax.all_to_all(layer_input[0].reshape(tokens, sequences, -1), "dp", 1, 0)
        own, far = wide[: sequences // 2], wide[sequences // 2 :]

    far_side, far_both, output = [], [], []

    def along_side(token):
        far_side.append(swap(after(far, token), side))
        output.extend(
            by_heads(
                local_output_head,
                [("held", after(query, token)), ("held", key), ("held", value)],
                [("held row", F32)],
                2,
            )
        )
        return far_side + output

    forward.spread([], [far], along_side, True)
    forward.collect()
    far_layer = swap(after(far, forward.before), layer)
    grad_output, block_grad, state_in = by_heads(
        functools.partial(grad_output_head, forward.counts),
        [("held", query), ("held", output[0]), ("held", upstream), *forward.operands],
        [("held row", BF16), ("held state", BF16), ("state", BF16)],
        2,
        bits,
    )
    own_layer = swap(after(own, block_grad), layer)
    backward = Scan(after(block_grad, far_layer), bits, True)
    own_side = swap(after(own, backward.mine), side)
    (key_local,) = by_heads(
        key_local_head,
        [("held", query), ("held", value), ("held", after(grad_output, backward.mine))],
        [("held row", F32)],
        2,
    )

    def along_side_again(token):
        far_both.append(swap(after(far_layer, token), side))
        return far_both

    backward.spread([key_local], [own_side, own_layer], along_side_again, False)
    backward.collect()
    own_both = swap(after(own_side, backward.before), layer)
    key_grad, *turned = by_heads(
        functools.partial(key_grad_head, backward.counts),
        [("held", after(key, own_both)), ("held", value), ("held", key_local), *backward.operands],
        [("row", BF16)] + [((sequences, 8, halves, rows, tokens), BF16)] * cuts,
        1,
        bits,
    )
    own_ids, far_ids = range(sequences // 2), range(sequences // 2, sequences)
    held, sources_of = [], []
    for array, ids, layered, sided in (
        (own, own_ids, 0, 0),
        (far, far_ids, 0, 0),
        (own_layer, own_ids, 1, 0),
        (far_layer, far_ids, 1, 0),
        (far_side[0], far_ids, 0, 1),
        (far_both[0], far_ids, 1, 1),
        (own_side, own_ids, 0, 1),
        (own_both, own_ids, 1, 1),
    ):
        held.append(array)
        sources_of.append((ids, (0, sided, layered)))
    held += [swap(array, core) for array in held]
    sources_of += [(ids, (1, sided, layered)) for ids, (_, sided, layered) in sources_of]
    turned[0] = after(turned[0], *held[8:])

    sums, done = [], turned[0]
    for cut in range(cuts):
        part = turned[cut].reshape(sequences * 8, halves * rows, tokens)
        part = lax.all_to_all(part, ("dp", layer, side, core), 0, 0, tiled=True)
        total, sent = weight_part(sources_of, bits, after(part, done), held, halves)
        if not sums:
            query_grad, value_grad = by_heads(
                functools.partial(other_grads_head, backward.counts),
                [
                    ("held", query),
                    ("held", key),
                    ("held", value),
                    ("held", after(grad_output, sent)),
                    ("state", state_in),
                    *backward.operands,
                ],
                [("row", BF16), ("row", BF16)],
                6,
                bits,
            )
        for turn in range(1, halves):
            moved = lax.ppermute(sent[turn - 1], spans, [(i, (i + turn) % halves) for i in range(halves)])
            total += moved.astype(F32)
        done = value_grad if not sums else sent
        sums.append(total)
    weight_grad = jnp.concatenate(sums) * (sequences * places * tokens) ** (-0.5)
    return (query_grad[None], key_grad[None], value_grad[None], weight_grad)


def solution(mesh):
    sequences, places = mesh.shape["dp"], mesh.shape["ctx"]
    bits = tuple(f"bit{i}" for i in range(places.bit_length() - 1))
    ctx = tuple(reversed(bits))
    devices = mesh.devices.reshape((sequences,) + (2,) * len(bits))
    rows = P("dp", ctx, None)
    return jax.shard_map(
        functools.partial(shards, bits=bits),
        mesh=jax.sharding.Mesh(devices, ("dp",) + ctx),
        in_specs=(rows,) * 5,
        out_specs=(rows, rows, rows, P(ctx, "dp")),
        check_vma=False,
    )
```

```python
import functools

import jax
import jax.numpy as jnp
from jax import lax
from jax.experimental import pallas as pl
from jax.experimental.pallas import tpu as pltpu
from jax.sharding import PartitionSpec as P

HEAD_DIM = 128
EPSILON = 1e-05
VMEM_MIB = 56
F32 = jnp.float32
BF16 = jnp.bfloat16

NN = (((1,), (0,)), ((), ()))
NT = (((1,), (1,)), ((), ()))
TN = (((0,), (0,)), ((), ()))


def dot(a, b, dims):
    return lax.dot_general(a, b, dims, preferred_element_type=F32)


def slope(values):
    wide = values.astype(F32)
    return jnp.where(wide > 0, 1.0, jnp.exp(jnp.minimum(wide, 0.0)))


def feature(values):
    wide = values.astype(F32)
    return jnp.where(wide > 0, wide + 1.0, jnp.exp(jnp.minimum(wide, 0.0))).astype(BF16)


def causal_scores(rows, columns):
    scores = dot(rows, columns, NT)
    t = lax.broadcasted_iota(jnp.int32, scores.shape, 0)
    s = lax.broadcasted_iota(jnp.int32, scores.shape, 1)
    return jnp.where(s <= t, scores, 0.0).astype(BF16)


def causal_scores_turned(rows, columns):
    scores = dot(columns, rows, NT)
    s = lax.broadcasted_iota(jnp.int32, scores.shape, 0)
    t = lax.broadcasted_iota(jnp.int32, scores.shape, 1)
    return jnp.where(s <= t, scores, 0.0).astype(BF16)


def block_state_head(at, k_ref, v_ref, state_ref):
    state_ref[at, :] = dot(feature(k_ref[:, at]), v_ref[:, at], TN).astype(BF16)


def local_output_head(at, q_ref, k_ref, v_ref, local_ref):
    scores = causal_scores(feature(q_ref[:, at]), feature(k_ref[:, at]))
    local_ref[:, at] = dot(scores, v_ref[:, at], NN)


def assemble(at, counts, flags_ref, other_ref, quarter_refs):
    size = quarter_refs[0].shape[0]
    quarter, start = divmod(at.start, size)
    near = flags_ref[0] == quarter // 2
    same = flags_ref[1] == quarter % 2
    own, other, swapped_own, swapped_other = [ref[start : start + HEAD_DIM, :] for ref in quarter_refs]
    total = jnp.where(same, jnp.where(near, own, swapped_own), jnp.where(near, other, swapped_other))
    return added_if(flags_ref[counts] == 1, total, other_ref[at, :])


def grad_output_head(counts, at, flags_ref, q_ref, local_ref, upstream_ref, other_ref, *refs):
    *quarter_refs, grad_ref, block_ref, state_ref = refs
    state = assemble(at, counts, flags_ref, other_ref, quarter_refs)
    state_ref[at, :] = state
    query = feature(q_ref[:, at])
    output = local_ref[:, at] + dot(query, state, NN)
    inverse_rms = lax.rsqrt(jnp.mean(output * output, axis=-1, keepdims=True) + EPSILON)
    normed = output * inverse_rms
    upstream = upstream_ref[:, at].astype(F32)
    projection = jnp.mean(upstream * normed, axis=-1, keepdims=True)
    grad = (inverse_rms * (upstream - normed * projection)).astype(BF16)
    grad_ref[:, at] = grad
    block_ref[at, :] = dot(query, grad, TN).astype(BF16)


def key_local_head(at, q_ref, v_ref, grad_ref, key_out):
    grad_scores = causal_scores_turned(grad_ref[:, at], v_ref[:, at])
    key_out[:, at] = dot(grad_scores, feature(q_ref[:, at]), NN)


def key_grad_head(counts, at, flags_ref, k_ref, v_ref, local_ref, other_ref, *refs):
    *quarter_refs, key_out = refs[:5]
    turned_out = refs[5:]
    cuts = len(turned_out)
    copies, devices, halves, rows, tokens = turned_out[0].shape
    state = assemble(at, counts, flags_ref, other_ref, quarter_refs)
    key = local_ref[:, at] + dot(v_ref[:, at], state, NT)
    key = (key * slope(k_ref[:, at])).astype(BF16)
    key_out[:, at] = key
    turned = key.T
    start = at.start
    while start < at.stop:
        block, row = divmod(start, rows)
        size = min(rows - row, at.stop - start)
        owner, cut = divmod(block, cuts)
        half, device = divmod(owner, devices)
        for copy in range(copies):
            turned_out[cut][copy, device, half, row : row + size] = turned[start - at.start : start - at.start + size]
        start += size


def other_grads_head(counts, at, flags_ref, q_ref, k_ref, v_ref, grad_ref, state_ref, other_ref, *refs):
    *quarter_refs, query_out, value_out = refs
    later = assemble(at, counts, flags_ref, other_ref, quarter_refs)
    grad = grad_ref[:, at]
    key = feature(k_ref[:, at])
    grad_scores = causal_scores(grad, v_ref[:, at])
    query = dot(grad_scores, key, NN) + dot(grad, state_ref[at, :], NT)
    query_out[:, at] = (query * slope(q_ref[:, at])).astype(BF16)
    scores = causal_scores_turned(feature(q_ref[:, at]), key)
    value = dot(scores, grad, NN) + dot(key, later, NN)
    value_out[:, at] = value.astype(BF16)


def by_heads(head, operands, outs, matmuls, bits=None, vmem=12):
    tokens, features = operands[0][1].shape
    groups = 2 if features % (2 * HEAD_DIM) == 0 else 1
    group = features // groups
    shapes = {"row": (tokens, features), "state": (features, HEAD_DIM)}
    shapes_held = {"held row": shapes["row"], "held state": shapes["state"]}
    kinds = [kind for kind, _ in operands] + [kind for kind, _ in outs]
    results = [
        jax.ShapeDtypeStruct(shapes.get(kind) or shapes_held.get(kind, kind), dtype) for kind, dtype in outs
    ]
    held = [kind == "held" or kind in shapes_held for kind in kinds]
    arrays = [array for _, array in operands] + results
    count = len(operands)

    def part(kind, ref, index):
        cut = pl.ds(index * group, group)
        return ref.at[:, cut] if kind == "row" else ref.at[cut, :]

    def body(*refs):
        numbers = [] if bits is None else [numbers_of(bits)]
        there, moved = refs[: len(kinds)], refs[-1]
        scratch = iter(refs[len(kinds) : -1])
        here = [ref if stays else next(scratch) for stays, ref in zip(held, there)]

        def copy(index, step):
            source, target = (there, here) if index < count else (here, there)
            source, target = source[index], target[index]
            if kinds[index] in shapes:
                source, target = part(kinds[index], source, step), part(kinds[index], target, step)
            return pltpu.make_async_copy(source, target, moved.at[index, step])

        def at_once(index, step):
            return step == (0 if index < count else groups - 1)

        def due(step, indices):
            moving = [index for index in indices if not held[index]]
            return [index for index in moving if kinds[index] in shapes or at_once(index, step)]

        ins, outputs = range(count), range(count, len(kinds))
        for step in range(groups):
            for index in due(step, ins):
                copy(index, step).start()
        for step in range(groups):
            for index in due(step, ins):
                copy(index, step).wait()
            for start in range(step * group, (step + 1) * group, HEAD_DIM):
                head(slice(start, start + HEAD_DIM), *numbers, *here)
            for index in due(step, outputs):
                copy(index, step).start()
        for step in range(groups):
            for index in due(step, outputs):
                copy(index, step).wait()

    anywhere = pl.BlockSpec(memory_space=pl.ANY)
    places = [pl.BlockSpec(memory_space=pltpu.VMEM) if stays else anywhere for stays in held]
    return pl.pallas_call(
        body,
        in_specs=places[:count],
        out_specs=places[count:],
        out_shape=results,
        scratch_shapes=[
            pltpu.VMEM(array.shape, array.dtype) for stays, array in zip(held, arrays) if not stays
        ]
        + [pltpu.SemaphoreType.DMA((len(kinds), groups))],
        compiler_params=pltpu.CompilerParams(vmem_limit_bytes=vmem * 1024 * 1024),
        cost_estimate=pl.CostEstimate(
            flops=2 * matmuls * tokens * features * HEAD_DIM,
            bytes_accessed=tokens * features * 2 * len(kinds),
            transcendentals=0,
        ),
    )(*[array for _, array in operands])


def swap(array, axis):
    return lax.ppermute(array, axis, [(0, 1), (1, 0)])


def numbers_of(bits):
    place = [lax.axis_index(bit) for bit in bits]
    span = sum(2**index * at for index, at in enumerate(place[3:]))
    return place + place + [1 - at for at in place] + [lax.axis_index("dp"), span]


def added_if(flag, a, b):
    return (a.astype(F32) + jnp.where(flag, b.astype(F32), 0.0)).astype(BF16)


def small(body, bits, arrays, outs):
    vmem = pl.BlockSpec(memory_space=pltpu.VMEM)
    result = jax.ShapeDtypeStruct(arrays[-1].shape[-2:], BF16)

    def kernel(*refs):
        values = body(numbers_of(bits), *refs[: len(arrays)])
        for ref, value in zip(refs[len(arrays) :], values):
            ref[...] = value

    return pl.pallas_call(
        kernel,
        in_specs=[vmem] * len(arrays),
        out_specs=[vmem] * outs,
        out_shape=[result] * outs,
        compiler_params=pltpu.CompilerParams(vmem_limit_bytes=4 * 1024 * 1024),
        cost_estimate=pl.CostEstimate(flops=0, bytes_accessed=1024, transcendentals=0),
    )(*arrays)


def after(array, *others):
    if not others:
        return array
    return lax.optimization_barrier((array,) + others)[0]


class Scan:
    def __init__(self, state, bits, backward):
        first, second, *self.rest = bits
        self.first, self.second = first, second
        self.bits, self.counts = bits, (2 if backward else 1) * len(bits)
        state = state.reshape(2, 2, -1, HEAD_DIM)
        self.other = swap(state, first)

        def quarters(flags, state, other):
            core, side = flags[0], flags[1]
            return [added_if(True, state[core, at], other[core, at]) for at in (1 - side, side)]

        self.theirs, self.mine = small(quarters, self.bits, [state, self.other], 2)
        self.arrived = swap(self.theirs, second)

    def spread(self, due, early, meanwhile, rest_early):
        counts = self.counts
        self.arrived = after(self.arrived, *due)

        def start(flags, mine, arrived):
            return [added_if(True, mine[...], arrived[...])]

        (total,) = small(start, self.bits, [self.mine, self.arrived], 1)
        self.rest_arrived = swap(after(self.mine, self.arrived), self.second)
        if rest_early:
            early = [self.rest_arrived, *early]
        before = None
        for index, bit in enumerate(self.rest, 2):
            last = bit == self.rest[-1]
            pieces = meanwhile(total) if last else list(early)
            arrived = after(swap(total, bit), *pieces)

            def first(flags, total, arrived):
                values = arrived[...], total[...]
                return [jnp.where(flags[counts + 2] == 1, values[0], 0.0), added_if(True, *values)]

            def middle(flags, total, arrived, before):
                value = added_if(flags[counts + index] == 1, before[...], arrived[...])
                return [value, added_if(True, total[...], arrived[...])]

            def final(flags, side, arrived, before):
                value = added_if(flags[counts + index] == 1, before[...], arrived[...])
                return [value, added_if(flags[counts + 1] == 1, value, side[...])]

            if before is None:
                before, total = small(first, self.bits, [total, arrived], 2)
            elif not last:
                before, total = small(middle, self.bits, [total, arrived, before], 2)
            else:
                self.before, self.own = small(final, self.bits, [self.arrived, arrived, before], 2)

    def collect(self):
        counts = self.counts

        def finish(flags, swapped, rest):
            return [added_if(flags[counts + 1] == 1, swapped[...], rest[...])]

        arrays = [swap(self.before, self.second), self.rest_arrived]
        (other,) = small(finish, self.bits, arrays, 1)
        quarters = [self.own, other, swap(self.own, self.first), swap(other, self.first)]
        self.operands = [("whole", self.other.reshape(-1, HEAD_DIM))]
        self.operands += [("held", quarter) for quarter in quarters]


def sides_kernel(in_ref, own_ref, gone_ref):
    columns = own_ref.shape[1]
    mine = lax.axis_index("dp")

    @pl.when(mine == 0)
    def _():
        own_ref[...] = in_ref[:, :columns]
        gone_ref[...] = in_ref[:, columns:]

    @pl.when(mine == 1)
    def _():
        own_ref[...] = in_ref[:, columns:]
        gone_ref[...] = in_ref[:, :columns]


def sides(array):
    rows, columns = array.shape
    tile = rows // 2
    out = jax.ShapeDtypeStruct((rows, columns // 2), array.dtype)
    return pl.pallas_call(
        sides_kernel,
        grid=(rows // tile,),
        in_specs=[pl.BlockSpec((tile, columns), lambda i: (i, 0))],
        out_specs=[pl.BlockSpec((tile, columns // 2), lambda i: (i, 0))] * 2,
        out_shape=[out, out],
        compiler_params=pltpu.CompilerParams(vmem_limit_bytes=VMEM_MIB * 1024 * 1024),
        cost_estimate=pl.CostEstimate(flops=0, bytes_accessed=4 * array.size, transcendentals=0),
    )(array)


def weight_kernel(sources_of, bits, turned_in, *refs):
    *numbers, mine, span = numbers_of(bits)
    order = []
    for sequences, flips in sources_of:
        device = 0
        for bit, flip in enumerate(flips):
            device += 2**bit * (1 - numbers[bit] if flip else numbers[bit])
        pair = turned_in.shape[0] == 16
        order += [8 * (lax.rem(mine + at, 2) if pair else at) + device for at in sequences]
    *held, kept_out, sent_out, total_ref, turned_ref, buffer_ref, kept_ref, sent_ref, arrival, departure = refs
    sources, _, tokens = turned_ref.shape
    others, rows, columns = sent_ref.shape
    turning = pltpu.make_async_copy(turned_in, turned_ref, arrival.at[len(held)])
    turning.start()
    copies, at = [], 0
    for index, ref in enumerate(held):
        count = ref.shape[0]
        copies.append(pltpu.make_async_copy(ref, buffer_ref.at[at : at + count], arrival.at[index]))
        copies[-1].start()
        at += count
    per_step, tile = 4, 768 if columns % 768 == 0 else columns
    steps = sources // per_step
    leaving = []
    turning.wait()
    for step in range(steps):
        for copy in copies[step * len(copies) // steps : (step + 1) * len(copies) // steps]:
            copy.wait()
        first = step * per_step
        lhs = jnp.concatenate([turned_ref[order[first + i]] for i in range(per_step)], axis=1)
        for index, start in enumerate(range(0, columns, tile)):
            cut = slice(start, start + tile)
            rhs = buffer_ref[first : first + per_step, :, cut].reshape(per_step * tokens, tile)
            product = dot(lhs, rhs, NN)
            total_ref[:, cut] = product if step == 0 else total_ref[:, cut] + product
            if step < steps - 1:
                continue
            kept_ref[:, cut] = total_ref[pl.ds(pl.multiple_of(span * rows, 16), rows), cut]
            for turn in range(others):
                target = lax.rem(span + turn + 1, others + 1)
                sent_ref[turn, :, cut] = total_ref[pl.ds(pl.multiple_of(target * rows, 16), rows), cut].astype(BF16)
            there = pl.ds(start, tile)
            leaving += [
                pltpu.make_async_copy(kept_ref.at[:, there], kept_out.at[:, there], departure.at[0, index]),
                pltpu.make_async_copy(sent_ref.at[:, :, there], sent_out.at[:, :, there], departure.at[1, index]),
            ]
            leaving[-2].start()
            leaving[-1].start()
    for copy in leaving:
        copy.wait()


def weight_part(sources_of, bits, turned, inputs, halves):
    sources, rows, tokens = turned.shape
    columns = inputs[0].shape[-1]
    return pl.pallas_call(
        functools.partial(weight_kernel, sources_of, bits),
        in_specs=[pl.BlockSpec(memory_space=pl.ANY)] * (1 + len(inputs)),
        out_specs=[pl.BlockSpec(memory_space=pl.ANY)] * 2,
        out_shape=[
            jax.ShapeDtypeStruct((rows // halves, columns), F32),
            jax.ShapeDtypeStruct((halves - 1, rows // halves, columns), BF16),
        ],
        scratch_shapes=[
            pltpu.VMEM((rows, columns), F32),
            pltpu.VMEM(turned.shape, BF16),
            pltpu.VMEM((sources, tokens, columns), BF16),
            pltpu.VMEM((rows // halves, columns), F32),
            pltpu.VMEM((halves - 1, rows // halves, columns), BF16),
            pltpu.SemaphoreType.DMA((len(inputs) + 1,)),
            pltpu.SemaphoreType.DMA((2, max(columns // 512, 1))),
        ],
        compiler_params=pltpu.CompilerParams(vmem_limit_bytes=VMEM_MIB * 1024 * 1024),
        cost_estimate=pl.CostEstimate(
            flops=2 * sources * tokens * rows * columns,
            bytes_accessed=sources * tokens * columns * 2 + rows * columns * 6,
            transcendentals=0,
        ),
    )(turned, *inputs)


def shards(layer_input, query_rows, key_rows, value_rows, out_grad, bits):
    query, key, value, upstream = query_rows[0], key_rows[0], value_rows[0], out_grad[0]
    tokens, features = query.shape
    sequences = lax.axis_size("dp")
    places = 2 ** len(bits)
    core, side, layer, *high = bits
    spans = tuple(reversed(high))
    halves = places // 8
    cuts = 2
    rows = features // places // cuts

    (block_state,) = by_heads(
        block_state_head, [("held", key), ("held", value)], [("held state", BF16)], 1
    )
    forward = Scan(block_state, bits, False)

    if sequences == 2:
        own, gone = sides(after(layer_input[0], forward.mine))
        own, far = own[None], swap(gone, "dp")[None]
    else:
        wide = lax.all_to_all(layer_input[0].reshape(tokens, sequences, -1), "dp", 1, 0)
        own, far = wide[: sequences // 2], wide[sequences // 2 :]

    far_side, far_both, output = [], [], []

    def along_side(token):
        far_side.append(swap(after(far, token), side))
        output.extend(
            by_heads(
                local_output_head,
                [("held", after(query, token)), ("held", key), ("held", value)],
                [("held row", F32)],
                2,
            )
        )
        return far_side + output

    forward.spread([], [far], along_side, True)
    forward.collect()
    far_layer = swap(after(far, forward.before), layer)
    grad_output, block_grad, state_in = by_heads(
        functools.partial(grad_output_head, forward.counts),
        [("held", query), ("held", output[0]), ("held", upstream), *forward.operands],
        [("held row", BF16), ("held state", BF16), ("state", BF16)],
        2,
        bits,
    )
    own_layer = swap(after(own, block_grad), layer)
    backward = Scan(after(block_grad, far_layer), bits, True)
    own_side = swap(after(own, backward.mine), side)
    (key_local,) = by_heads(
        key_local_head,
        [("held", query), ("held", value), ("held", after(grad_output, backward.mine))],
        [("held row", F32)],
        2,
    )

    def along_side_again(token):
        far_both.append(swap(after(far_layer, token), side))
        return far_both

    backward.spread([key_local], [own_side, own_layer], along_side_again, False)
    backward.collect()
    own_both = swap(after(own_side, backward.before), layer)
    key_grad, *turned = by_heads(
        functools.partial(key_grad_head, backward.counts),
        [("held", after(key, own_both)), ("held", value), ("held", key_local), *backward.operands],
        [("row", BF16)] + [((sequences, 8, halves, rows, tokens), BF16)] * cuts,
        1,
        bits,
    )
    own_ids, far_ids = range(sequences // 2), range(sequences // 2, sequences)
    held, sources_of = [], []
    for array, ids, layered, sided in (
        (own, own_ids, 0, 0),
        (far, far_ids, 0, 0),
        (own_layer, own_ids, 1, 0),
        (far_layer, far_ids, 1, 0),
        (far_side[0], far_ids, 0, 1),
        (far_both[0], far_ids, 1, 1),
        (own_side, own_ids, 0, 1),
        (own_both, own_ids, 1, 1),
    ):
        held.append(array)
        sources_of.append((ids, (0, sided, layered)))
    held += [swap(array, core) for array in held]
    sources_of += [(ids, (1, sided, layered)) for ids, (_, sided, layered) in sources_of]
    turned[0] = after(turned[0], *held[8:])

    sums, done = [], turned[0]
    for cut in range(cuts):
        part = turned[cut].reshape(sequences * 8, halves * rows, tokens)
        part = lax.all_to_all(part, ("dp", layer, side, core), 0, 0, tiled=True)
        total, sent = weight_part(sources_of, bits, after(part, done), held, halves)
        if not sums:
            query_grad, value_grad = by_heads(
                functools.partial(other_grads_head, backward.counts),
                [
                    ("held", query),
                    ("held", key),
                    ("held", value),
                    ("held", after(grad_output, sent)),
                    ("state", state_in),
                    *backward.operands,
                ],
                [("row", BF16), ("row", BF16)],
                6,
                bits,
            )
        for turn in range(1, halves):
            moved = lax.ppermute(sent[turn - 1], spans, [(i, (i + turn) % halves) for i in range(halves)])
            total += moved.astype(F32)
        done = value_grad if not sums else sent
        sums.append(total)
    weight_grad = jnp.concatenate(sums) * (sequences * places * tokens) ** (-0.5)
    return (query_grad[None], key_grad[None], value_grad[None], weight_grad)


def solution(mesh):
    sequences, places = mesh.shape["dp"], mesh.shape["ctx"]
    bits = tuple(f"bit{i}" for i in range(places.bit_length() - 1))
    ctx = tuple(reversed(bits))
    devices = mesh.devices.reshape((sequences,) + (2,) * len(bits))
    rows = P("dp", ctx, None)
    return jax.shard_map(
        functools.partial(shards, bits=bits),
        mesh=jax.sharding.Mesh(devices, ("dp",) + ctx),
        in_specs=(rows,) * 5,
        out_specs=(rows, rows, rows, P(ctx, "dp")),
        check_vma=False,
    )
```
